32 devices in a mesh: view: 8 (over z, core), slab: 4 (over y, x).
Axes of the slice: x: 2, y: 2, z: 4, core: 2. Of those that a mesh axis runs over, the one named last changes fastest.
Arguments:
- latent: bfloat16 [32, 32, 1024], P(None, 'slab'), may hold values from -6 to 6
- tconv_weight: bfloat16 [32, 32, 8], replicated, may hold values from -1 to 1
- depth_weight: float32 [32, 27], replicated, may hold values from -2 to 2
- point_weight: bfloat16 [4, 32], replicated, may hold values from -1 to 1
- pencil_ids: int32 [8, 1024], P('view'), may hold values from 0 to 4095, as said below
- targets: float32 [8, 3, 1024], P('view', None, 'slab'), may hold values from 0 to 1
Outputs:
- colours: float32 [8, 3, 1024], P('view', None, 'slab')
- latent_grad: float32 [32, 32, 1024], P(None, 'slab')
The draws below stay inside these ranges and needn't reach their ends.
Inputs may be any that keep to these rules, and one draw needn't show every extreme that they name: `pencil_ids`: within one view group the ids are distinct; every view group names cell 0 and cell 4 * 32 * 32 - 1.
All inputs are finite; a program needn't handle non-finite values.
Results may differ from the reference program's by a relative error of at most 0.005.
Values may be sent and summed in bfloat16 or wider, within the bound.
No kernel may reach another device: no remote copies, remote signals or barrier semaphores. Data moves between devices by JAX's collectives and lax.ppermute only.
A program may use at most 192 MiB of HBM per device.

```python
import jax
import jax.numpy as jnp
from jax import lax

C = 32
CX = 32
CY = 32
VIEWS = 8
NZC = 32
PENCILS = 1024


def draw_pencil_ids(key, part):
    key = jax.random.fold_in(key, 7)
    cells = 4 * CX * CY
    keys = jax.random.split(key, VIEWS)

    def one_group(group_key):
        first_key, second_key = jax.random.split(group_key)
        others = 1 + jax.random.permutation(first_key, cells - 2)[:PENCILS - 2]
        ends = jnp.array([0, cells - 1], jnp.int32)
        joined = jnp.concatenate([ends, others.astype(jnp.int32)])
        return jax.random.permutation(second_key, joined).astype(jnp.int32)
    return jax.vmap(one_group)(keys)


def levels(stream_key, dims, cuts, low, top_value):
    loudness = 1.0
    for axis_at, blocks in cuts:
        heights = jax.random.uniform(jax.random.fold_in(jax.random.fold_in(stream_key, 6), axis_at), (blocks,), jnp.float32, low / len(cuts), top_value / len(cuts))
        loudness = loudness * jnp.repeat(jnp.exp(heights), dims[axis_at] // blocks).reshape((-1,) + (1,) * (len(dims) - 1 - axis_at))
    return loudness


def centred(rng, extent, spread, limit, cuts=(), kind=jnp.bfloat16):
    gain = levels(rng, extent, cuts, -0.22, 0.18) if cuts else 1.0
    values = jax.random.normal(rng, extent, jnp.float32) * spread * gain
    return jnp.minimum(jnp.maximum(values, -limit), limit).astype(kind)


def setup_inputs(seed: int = 0) -> dict:
    arg_keys = jax.random.split(jax.random.key(seed), 7)
    latent = centred(arg_keys[0], (C, NZC, CX * CY), 1.0, 6.0, ((1, 4),))
    tconv_weight = centred(arg_keys[1], (C, C, 8), C ** -0.5, 1.0)
    depth_weight = centred(arg_keys[2], (C, 27), 9 ** -0.5, 2.0, (), jnp.float32)
    point_weight = centred(arg_keys[3], (4, C), C ** -0.5, 1.0)
    pencil_ids = draw_pencil_ids(jax.random.fold_in(arg_keys[6], 71), 0)
    targets = jnp.clip(1.0 * jax.random.uniform(arg_keys[5], (VIEWS, 3, PENCILS), jnp.float32) ** levels(arg_keys[5], (VIEWS, 3, PENCILS), ((0, 8), (2, 4)), -0.2, 0.2), 0.0, 1.0)
    return dict(latent=latent, tconv_weight=tconv_weight, depth_weight=depth_weight, point_weight=point_weight, pencil_ids=pencil_ids, targets=targets)


def decode_grid(latent, tconv_weight):
    chans = latent.shape[0]
    depth = latent.shape[1]
    grid4 = latent.reshape(chans, depth, CX, CY).astype(jnp.float32)
    weight5 = tconv_weight.reshape(chans, chans, 2, 2, 2).astype(jnp.float32)
    fine = jnp.einsum('izxy,ioabc->ozaxbyc', grid4, weight5)
    return fine.reshape(chans, 2 * depth, 4 * CX * CY).astype(jnp.bfloat16)

def depthwise_apply(padded, depth_weight, flipped):
    chans = padded.shape[0]
    depth = padded.shape[1] - 2
    grid4 = padded.reshape(chans, depth + 2, 2 * CX, 2 * CY)
    grid4 = jnp.pad(grid4, ((0, 0), (0, 0), (1, 1), (1, 1)))
    total = jnp.zeros((chans, depth, 2 * CX, 2 * CY), jnp.float32)
    for first in range(3):
        for second in range(3):
            for third in range(3):
                coeff = depth_weight[:, 9 * first + 3 * second + third][:, None, None, None]
                if flipped:
                    sa, sb, sc = (2 - first, 2 - second, 2 - third)
                else:
                    sa, sb, sc = (first, second, third)
                total = total + coeff * grid4[:, sa:sa + depth, sb:sb + 2 * CX, sc:sc + 2 * CY].astype(jnp.float32)
    return total.reshape(chans, depth, 4 * CX * CY)

def composite(raw):
    steps_count = raw.shape[1]
    sigma = jax.nn.softplus(raw[0])
    colour = jax.nn.sigmoid(raw[1:4])
    optical = sigma * (1.5 / steps_count)
    before = jnp.cumsum(optical, axis=0) - optical
    weights = jnp.exp(-before) * (1.0 - jnp.exp(-optical))
    return lax.optimization_barrier(jnp.sum(weights[None] * colour, axis=1))

def latent_back(grad_fine, tconv_weight, depth):
    chans = grad_fine.shape[0]
    grad7 = grad_fine.reshape(chans, depth, 2, CX, 2, CY, 2)
    weight5 = tconv_weight.reshape(chans, chans, 2, 2, 2).astype(jnp.float32)
    result = jnp.einsum('ozaxbyc,ioabc->izxy', grad7, weight5, precision=lax.Precision.HIGHEST)
    return result.reshape(chans, depth, CX * CY)

def reference(latent, tconv_weight, depth_weight, point_weight, pencil_ids, targets):
    fine = decode_grid(latent, tconv_weight)
    padded = jnp.pad(fine, ((0, 0), (1, 1), (0, 0)))
    depthwise = depthwise_apply(padded, depth_weight, False)
    features = jax.nn.silu(depthwise).astype(jnp.bfloat16)
    raw = jnp.einsum('oc,czp->ozp', point_weight.astype(jnp.float32), features.astype(jnp.float32))

    def one_view(total, item):
        ids, target = item
        picked = jnp.take(raw, ids, axis=2)
        colour, back = jax.vjp(composite, picked)
        grad_pick, = back(colour - target)
        return (total.at[:, :, ids].add(grad_pick), colour)
    start = jnp.zeros(raw.shape, jnp.float32)
    grad_raw, colours = lax.scan(one_view, start, (pencil_ids, targets))
    grad_features = jnp.einsum('oc,ozp->czp', point_weight.astype(jnp.float32), grad_raw, precision=lax.Precision.HIGHEST)
    sig = jax.nn.sigmoid(depthwise)
    grad_depthwise = grad_features * sig * (1.0 + depthwise * (1.0 - sig))
    grad_padded = jnp.pad(grad_depthwise, ((0, 0), (1, 1), (0, 0)))
    grad_fine = depthwise_apply(grad_padded, depth_weight, True)
    latent_grad = latent_back(grad_fine, tconv_weight, latent.shape[1])
    return (colours, latent_grad)
```

```python
import functools

import jax
import jax.numpy as jnp
from jax import lax
from jax.experimental import pallas as pl
from jax.experimental.pallas import tpu as pltpu
from jax.sharding import PartitionSpec as P

CX = 32
CY = 32
F32 = jnp.float32
BF16 = jnp.bfloat16
VMEM_LIMIT = 24 * 1024 * 1024
VM = pl.BlockSpec(memory_space=pltpu.VMEM)
SM = pl.BlockSpec(memory_space=pltpu.SMEM)


def rows_of(split):
    if split == 1:
        return CX
    return min(CX, -(-(CX // split + 1) // 4) * 4)


def lane_shift(x, amount, y):
    width = x.shape[-1]
    moved = pltpu.roll(x, (-amount) % width, 1)
    if amount == 1:
        keep = y < CY - 1
    elif amount == -1:
        keep = y > 0
    else:
        lane = lax.broadcasted_iota(jnp.int32, x.shape, 1)
        keep = lane < width - CY if amount > 0 else lane >= CY
    return jnp.where(keep, moved, 0.0)


def thirds(x):
    high = x.astype(BF16)
    rest = x - high.astype(F32)
    mid = rest.astype(BF16)
    low = (rest - mid.astype(F32)).astype(BF16)
    return jnp.concatenate([high, mid, low], axis=0)


def softplus(x):
    return jnp.maximum(x, 0.0) + jnp.log1p(jnp.exp(-jnp.abs(x)))


def swap(x):
    return pltpu.roll(x, 4, 0)


def spread(x, put):
    chans, width = x.shape
    lane = lax.broadcasted_iota(jnp.int32, (chans, width), 1)

    def keep(inside):
        return jnp.where(inside, 1.0, 0.0).astype(BF16)

    before = pltpu.roll(x * keep(lane % CY != CY - 1), 1, 1)
    after = pltpu.roll(x * keep(lane % CY != 0), width - 1, 1)
    for j, by_y in enumerate((before, x, after)):
        put(chans * j, pltpu.roll(by_y * keep(lane < width - CY), CY, 1))
        put(chans * (3 + j), by_y)
        put(chans * (6 + j), pltpu.roll(by_y * keep(lane >= CY), width - CY, 1))


def composed(taps_ref, weight, e):
    total = None
    for a in range(2):
        for b in range(2):
            for c in range(2):
                d = (a + 2 - e[0], b + 2 - e[1], c + 2 - e[2])
                if min(d) >= 0 and max(d) <= 2:
                    term = weight(9 * d[0] + 3 * d[1] + d[2]) * taps_ref[4 * a + 2 * b + c]
                    total = term if total is None else total + term
    return total


def near(parity):
    return (-1, 0) if parity == 0 else (0, 1)


def decode_pair(layers, wide_ref, point, slope_ref, raw_ref, k):
    chans = wide_ref.shape[1] // 4
    features = []
    for b in range(2):
        for c in range(2):
            around = jnp.concatenate(
                [
                    layers[j](chans * (3 * (nx + 1) + ny + 1))
                    for j in range(2)
                    for nx in near(b)
                    for ny in near(c)
                ],
                axis=0,
            )
            dw = jnp.dot(wide_ref[2 * b + c], around, preferred_element_type=F32)
            dw = dw[: 2 * chans] + dw[2 * chans :]
            sig = jax.nn.sigmoid(dw)
            silu = dw * sig
            row = 2 * chans * (2 * b + c)
            slope_ref[k, row : row + 2 * chans, :] = silu + sig * (1.0 - silu)
            features.append(silu.astype(BF16))
    raw_ref[k] = jnp.dot(point, jnp.concatenate(features, axis=0), preferred_element_type=F32)


def weight_kernel(taps_ref, depth_ref, wide_ref, full_ref):
    chans = taps_ref.shape[1]
    columns = [jnp.broadcast_to(depth_ref[:, i : i + 1], (chans, chans)) for i in range(27)]
    for b in range(2):
        for c in range(2):
            for first in range(2):
                for j in range(2):
                    for nx in near(b):
                        for ny in near(c):
                            e = (2 - 2 * j + first, b - 2 * nx + 1, c - 2 * ny + 1)
                            at = chans * (4 * j + 2 * (nx - near(b)[0]) + ny - near(c)[0])
                            full_ref[2 * b + c, chans * first : chans * (first + 1), at : at + chans] = composed(
                                taps_ref, lambda i: columns[i], e
                            )
    high = full_ref[...].astype(BF16)
    wide_ref[:, : 2 * chans, :] = high
    wide_ref[:, 2 * chans :, :] = (full_ref[...] - high.astype(F32)).astype(BF16)


def turn_kernel(taps_ref, depth_ref, wide_ref, full_ref):
    chans = taps_ref.shape[1]
    full_ref[...] = jnp.zeros_like(full_ref)
    columns = [jnp.broadcast_to(depth_ref[:, i : i + 1], (chans, chans)) for i in range(27)]
    for b in range(2):
        for n in range(2):
            nx = n - b
            for ny in (-1, 0, 1):
                col = chans * (3 * n + ny + 1)
                for j in range(4):
                    for c in range(2):
                        e = (j, 2 * nx + b + 1, 2 * ny + c + 1)
                        if 0 <= e[2] < 4:
                            row = chans * (4 * (j // 2) + 2 * c + j % 2)
                            full_ref[b, row : row + chans, col : col + chans] = composed(
                                taps_ref, lambda i: columns[i], e
                            )
        wide_ref[b] = full_ref[b].T[: 6 * chans].astype(BF16)


def inner_kernel(lat_ref, wide_ref, point_ref, away_ref, raw_ref, edge_ref, x9_ref, slope_ref, sems):
    layers, chans, width = lat_ref.shape


    def layer(k):
        def put(at, block):
            x9_ref[k, at : at + chans, :] = block

        spread(lat_ref[k], put)

    layer(0)
    for k in range(layers - 1):
        layer(k + 1)
        around = [lambda at, j=j: x9_ref[k + j, at : at + chans, :] for j in range(2)]
        decode_pair(around, wide_ref, point_ref[...], slope_ref, raw_ref, k)
        pltpu.make_async_copy(slope_ref.at[k], away_ref.at[k], sems.at[k]).start()
    edge_ref[0] = x9_ref[0]
    edge_ref[1] = x9_ref[layers - 1]
    for k in range(layers - 1):
        pltpu.make_async_copy(slope_ref.at[k], away_ref.at[k], sems.at[k]).wait()


def outer_kernel(
    scale, where_ref, one_ref, two_ref, edge_ref, wide_ref, point_ref, inner_ref,
    slope_ref, raw_ref, tot_ref, x9_ref,
):
    slab, slabs = where_ref[0], where_ref[3]
    width = one_ref.shape[1]
    chans = edge_ref.shape[1] // 9
    pairs = inner_ref.shape[0] + 2
    even = lax.rem(slab, 2) == 0
    one, two = one_ref[0:chans, :], two_ref[0:chans, :]
    low = jnp.where(slab == 0, 0.0, jnp.where(even, two, one))
    high = jnp.where(slab == slabs - 1, 0.0, jnp.where(even, one, two))
    for k, x in ((0, low), (1, high)):

        def put(at, block, k=k):
            x9_ref[k, at : at + chans, :] = block

        spread(x.astype(BF16), put)
        layers = [lambda at, k=k: x9_ref[k, at : at + chans, :], lambda at, k=k: edge_ref[k, at : at + chans, :]]
        decode_pair(layers if k == 0 else layers[::-1], wide_ref, point_ref[...], slope_ref, raw_ref, k)
    second = lax.broadcasted_iota(jnp.int32, (8, width), 0) >= 4
    before = jnp.zeros((8, width), F32)
    colour = [jnp.zeros((8, width), F32) for _ in range(3)]
    for k in range(pairs):
        raw = raw_at(raw_ref, inner_ref, k)
        tau = softplus(raw[0:8]) * scale
        if k == 0:
            tau = jnp.where(second, tau, 0.0)
        if k == pairs - 1:
            tau = jnp.where(second, 0.0, tau)
        other = swap(tau)
        weight = jnp.exp(-(before + jnp.where(second, other, 0.0))) * (1.0 - jnp.exp(-tau))
        before = before + (tau + other)
        for o in range(3):
            colour[o] = colour[o] + weight * jax.nn.sigmoid(raw[8 * o + 8 : 8 * o + 16])
    colour = [c + swap(c) for c in colour]
    tot_ref[0:8, :] = jnp.where(second, colour[0], before)
    tot_ref[8:16, :] = jnp.where(second, colour[2], colour[1])


def raw_at(outer_ref, inner_ref, k):
    last = inner_ref.shape[0] + 1
    if k == 0:
        return outer_ref[0]
    if k == last:
        return outer_ref[1]
    return inner_ref[k - 1]


def cell_of(ids):
    fine_x, fine_y = ids // (2 * CY), ids % (2 * CY)
    return (fine_x // 2) * CY + fine_y // 2, (fine_x % 2) * 2 + fine_y % 2


def target_kernel(where_ref, tot_ref, own_ref, other_ref, msg_ref):
    width = tot_ref.shape[1]
    start = where_ref[1]
    msg_ref[0:16, :] = tot_ref[...]
    count = own_ref.shape[1]
    row = lax.broadcasted_iota(jnp.int32, (16, count), 0)
    cells = lax.broadcasted_iota(jnp.int32, (count, width), 1)
    total = jnp.zeros((48, width), F32)
    for ref in (own_ref, other_ref):
        for j in range(ref.shape[0] // 4):
            block = ref[4 * j : 4 * j + 4, :]
            cell, part = cell_of(block[3:4, :].astype(jnp.int32))
            value = jnp.where(row < 4, 1.0, jnp.where(row < 8, block[0:1, :], jnp.where(row < 12, block[1:2, :], block[2:3, :])))
            value = jnp.where(row % 4 == part, value, 0.0)
            column = jnp.broadcast_to(cell - start, (8, count)).astype(F32).T[:, 0:1].astype(jnp.int32)
            hot = jnp.where(cells == column, 1.0, 0.0).astype(BF16)
            total = total + jnp.dot(thirds(value), hot, preferred_element_type=F32)
    msg_ref[16:32, :] = total[0:16] + (total[16:32] + total[32:48])


def back_kernel(scale, where_ref, *refs):
    (*msg_refs, inner_ref, outer_ref, away_ref, slope2_ref, wide_ref, point_ref, near_ref) = refs[:-8]
    grad_ref, colour_ref, gdw_ref, e_ref, w_ref, tile_ref, slope_ref, sems = refs[-8:]
    slab, start, own_start = where_ref[0], where_ref[1], where_ref[2]
    slabs = len(msg_refs)
    inner, _, width = inner_ref.shape
    pairs = inner + 2
    chans = slope_ref.shape[1] // 8
    own_width = grad_ref.shape[1]
    second = lax.broadcasted_iota(jnp.int32, (8, width), 0) >= 4
    for k in range(inner):
        pltpu.make_async_copy(away_ref.at[k], slope_ref.at[k], sems.at[k]).start()

    def both(x):
        other = swap(x)
        return jnp.where(second, other, x), jnp.where(second, x, other)

    totals, colours, hits = [], [], None
    for ref in msg_refs:
        tau_total, c0 = both(ref[0:8, :])
        c1, c2 = both(ref[8:16, :])
        totals.append(tau_total)
        colours.append((c0, c1, c2))
        here = (ref[16:24, :], ref[24:32, :])
        hits = here if hits is None else (hits[0] + here[0], hits[1] + here[1])
    index = [lax.rem(slab - k + slabs, slabs) for k in range(slabs)]
    full = [jnp.zeros((8, width), F32) for _ in range(3)]
    after = [jnp.zeros((8, width), F32) for _ in range(3)]
    prefix = None
    for k in range(slabs):
        ahead = jnp.zeros((8, width), F32)
        for other in range(slabs):
            if other != k:
                ahead = ahead + jnp.where(index[other] < index[k], totals[other], 0.0)
        if k == 0:
            prefix = ahead
        through = jnp.exp(-ahead)
        for o in range(3):
            part = through * colours[k][o]
            full[o] = full[o] + part
            if k:
                after[o] = after[o] + jnp.where(index[k] > slab, part, 0.0)
    number, t0 = both(hits[0])
    t1, t2 = both(hits[1])
    pull = [number * full[o] - t for o, t in enumerate((t0, t1, t2))]

    tau0 = softplus(outer_ref[0, 0:8, :]) * scale
    before = -both(tau0)[0]
    for k in range(pairs):
        tau = softplus(raw_at(outer_ref, inner_ref, k)[0:8]) * scale
        other = swap(tau)
        through = jnp.exp(-(prefix + (before + jnp.where(second, other, 0.0))))
        before = before + (tau + other)
        left = jnp.exp(-tau)
        w_ref[k, 0:8, :] = through * (1.0 - left)
        w_ref[k, 8:16, :] = through * left
    last = pairs - 1
    for o in range(3):
        e = w_ref[last, 0:8, :] * jax.nn.sigmoid(outer_ref[1, 8 * o + 8 : 8 * o + 16, :])
        after[o] = after[o] - both(e)[1]
    for k in range(pairs - 1, -1, -1):
        weight, later = w_ref[k, 0:8, :], w_ref[k, 8:16, :]
        raw = raw_at(outer_ref, inner_ref, k)
        total = jnp.zeros((8, width), F32)
        outside = None
        if k == 0:
            outside = jnp.logical_and(jnp.logical_not(second), slab == 0)
        if k == last:
            outside = jnp.logical_and(second, slab == slabs - 1)
        for o in range(3):
            rgb = jax.nn.sigmoid(raw[8 * o + 8 : 8 * o + 16])
            e = weight * rgb
            other = swap(e)
            rest = after[o] + jnp.where(second, 0.0, other)
            after[o] = after[o] + (e + other)
            total = total + pull[o] * (later * rgb - rest)
            grad = pull[o] * (e * (1.0 - rgb))
            if outside is not None:
                grad = jnp.where(outside, 0.0, grad)
            e_ref[k, 8 * o + 8 : 8 * o + 16, :] = grad
        grad = total * (scale * jax.nn.sigmoid(raw[0:8]))
        if outside is not None:
            grad = jnp.where(outside, 0.0, grad)
        e_ref[k, 0:8, :] = grad

    count = near_ref.shape[1]
    cell, part = cell_of(near_ref[...])
    cell = cell - own_start
    mine = jnp.logical_and(cell >= 0, cell < own_width)
    cell = jnp.where(mine, cell + (own_start - start), -1)
    hot = jnp.where(lax.broadcasted_iota(jnp.int32, (width, count), 0) == cell, 1.0, 0.0).astype(BF16)
    rows = jnp.concatenate(
        [jnp.where(second, full[1], full[0]), jnp.where(second, full[2], full[2])], axis=0
    )
    found = jnp.dot(thirds(rows), hot, preferred_element_type=F32)
    found = found[0:16] + (found[16:32] + found[32:48])
    row = lax.broadcasted_iota(jnp.int32, (16, count), 0)
    found = jnp.where(row % 4 == part, found, 0.0)
    for o in range(3):
        colour_ref[o : o + 1, :] = jnp.sum(found[4 * o : 4 * o + 4], axis=0, keepdims=True)

    def pair(k):
        if 0 < k < last:
            pltpu.make_async_copy(away_ref.at[k - 1], slope_ref.at[k - 1], sems.at[k - 1]).wait()
            slope = slope_ref[k - 1]
        else:
            slope = slope2_ref[k // last]
        grad_features = jnp.dot(point_ref[...], thirds(e_ref[k]), preferred_element_type=F32)
        gdw_ref[k] = (grad_features * slope).astype(BF16)

    y = lax.broadcasted_iota(jnp.int32, (chans, width), 1) % CY
    low = own_start == start
    for k in (0, last, *range(1, last)):
        pair(k)
    for z in range(pairs - 1):
        every = []
        for b in range(2):
            at = 4 * chans * b
            around = gdw_ref[z : z + 2, at : at + 4 * chans, :].reshape(8 * chans, width)
            every.append(jnp.dot(wide_ref[b], around, preferred_element_type=F32))
        total = None
        for j in range(3):
            at = chans * j
            line = every[0][at : at + chans] + every[1][at + 3 * chans : at + 4 * chans]
            line = line + lane_shift(every[1][at : at + chans], -CY, y)
            line = line + lane_shift(every[0][at + 3 * chans : at + 4 * chans], CY, y)
            if j != 1:
                line = lane_shift(line, j - 1, y)
            total = line if total is None else total + line
        if own_width < width:
            total = jnp.where(low, total[:, :own_width], total[:, width - own_width :])
        for t in range(own_width // 128):
            tile_ref[t, pl.ds(z, chans, stride=pairs - 1), :] = total[:, 128 * t : 128 * t + 128]
    for t in range(own_width // 128):
        grad_ref[:, 128 * t : 128 * t + 128] = tile_ref[t]


def call(kernel, outs, scratch, operands, smem, away_in=None, away_out=None):
    operands = list(operands)
    specs = [SM] * smem + [VM] * (len(operands) - smem)
    out_specs = [VM] * len(outs)
    shapes = [jax.ShapeDtypeStruct(s, t) for s, t in outs]
    if away_in is not None:
        operands[away_in] = pltpu.with_memory_space_constraint(operands[away_in], pltpu.HBM)
        specs[away_in] = pl.BlockSpec(memory_space=pltpu.HBM)
    if away_out is not None:
        shapes[away_out] = pltpu.HBM(*outs[away_out])
        out_specs[away_out] = pl.BlockSpec(memory_space=pltpu.HBM)
    return pl.pallas_call(
        kernel,
        out_shape=shapes,
        in_specs=specs,
        out_specs=out_specs,
        scratch_shapes=[pltpu.VMEM(*x) if isinstance(x, tuple) else x for x in scratch],
        compiler_params=pltpu.CompilerParams(vmem_limit_bytes=VMEM_LIMIT),
    )(*operands)


def on_device(latent, tconv_weight, depth_weight, point_weight, pencil_ids, targets):
    chans, depth, cells = latent.shape
    view, slab = lax.axis_index("view"), lax.axis_index("slab")
    views, slabs = lax.axis_size("view"), lax.axis_size("slab")
    count = targets.shape[2]
    split = 2 if views % 2 == 0 else 1
    rows = rows_of(split)
    width, own_width = rows * CY, cells // split
    half = view % split
    start = half * (cells - width)
    own_start = half * own_width
    where = jnp.stack([slab, start, own_start, slabs]).astype(jnp.int32)
    scale = 1.5 / (2 * depth * slabs)

    window = lax.dynamic_slice_in_dim(jnp.transpose(latent, (1, 0, 2)), start, width, axis=2)
    even = slab % 2 == 0
    first, last = window[0].astype(F32), window[depth - 1].astype(F32)
    ids = lax.dynamic_slice_in_dim(pencil_ids, slab * count, count, axis=1)
    blocks = jnp.concatenate([targets[0], ids.astype(F32)], axis=0)

    def widened(x):
        return jnp.pad(x, ((0, 0), (0, width - count)))

    def send(x, mask, partner):
        pairs = [(v * slabs + s, (v ^ mask) * slabs + partner(s)) for v in range(views) for s in range(slabs)]
        return lax.ppermute(x, ("view", "slab"), pairs)

    taps = jnp.transpose(tconv_weight.astype(F32), (2, 1, 0))
    eye = jnp.eye(8, dtype=BF16)
    point = point_weight[:, None, None, :] * eye[None, :, :, None]
    point = jnp.transpose(point.reshape(4, 8, 2, 4, chans), (0, 1, 3, 2, 4)).reshape(32, 8 * chans)
    point_back = jnp.tile(point.T, (1, 3))
    (wide,) = call(
        weight_kernel,
        [((4, 4 * chans, 8 * chans), BF16)],
        [((4, 2 * chans, 8 * chans), F32)],
        (taps, depth_weight),
        0,
    )
    (turned,) = call(
        turn_kernel,
        [((2, 6 * chans, 8 * chans), BF16)],
        [((2, 8 * chans, 8 * chans), F32)],
        (taps, depth_weight),
        0,
    )

    masks = [split << k for k in range((views // split).bit_length() - 1)]
    one = send(
        jnp.concatenate([jnp.where(even, last, first), widened(blocks)], axis=0),
        masks[0] if masks else 0,
        lambda s: (s + 1 - 2 * (s % 2)) % slabs,
    )
    one, wide, turned = lax.optimization_barrier((one, wide, turned))
    if masks:
        blocks = jnp.concatenate([blocks, one[chans:, :count]], axis=0)
    two = send(
        jnp.concatenate([jnp.where(even, first, last), widened(blocks)], axis=0),
        masks[1] if len(masks) > 1 else 0,
        lambda s: (s + 2 * (s % 2) - 1) % slabs,
    )
    inner = depth - 1
    slope, raw, edge = call(
        inner_kernel,
        [((inner, 8 * chans, width), F32), ((inner, 32, width), F32), ((2, 9 * chans, width), BF16)],
        [
            ((depth, 9 * chans, width), BF16),
            ((inner, 8 * chans, width), F32),
            pltpu.SemaphoreType.DMA((inner,)),
        ],
        (window, wide, point),
        0,
        away_out=0,
    )
    two, raw, edge = lax.optimization_barrier((two, raw, edge))
    if len(masks) > 1:
        blocks = jnp.concatenate([blocks, two[chans:, :count]], axis=0)
    for mask in masks[2:]:
        blocks = jnp.concatenate([blocks, send(blocks, mask, lambda s: s)], axis=0)
    own_blocks = blocks
    if split == 2:
        pairing = [(i, i ^ 1) for i in range(views)]
        other_blocks = lax.ppermute(own_blocks, "view", pairing)
        near_ids = jnp.concatenate([ids, other_blocks[3:4].astype(jnp.int32)], axis=1)
    else:
        other_blocks, near_ids = own_blocks[:0], ids
    slope2, raw2, tot = call(
        functools.partial(outer_kernel, scale),
        [((2, 8 * chans, width), F32), ((2, 32, width), F32), ((16, width), F32)],
        [((2, 9 * chans, width), BF16)],
        (where, one, two, edge, wide, point, raw),
        1,
    )
    (message,) = call(target_kernel, [((32, width), F32)], [], (where, tot, own_blocks, other_blocks), 1)
    messages = [message]
    for k in range(1, slabs):
        messages.append(lax.ppermute(message, "slab", [(i, (i + k) % slabs) for i in range(slabs)]))
    grad, found = call(
        functools.partial(back_kernel, scale),
        [((chans * depth, own_width), F32), ((3, split * count), F32)],
        [
            ((inner + 2, 8 * chans, width), BF16),
            ((inner + 2, 32, width), F32),
            ((inner + 2, 16, width), F32),
            ((own_width // 128, chans * depth, 128), F32),
            ((inner, 8 * chans, width), F32),
            pltpu.SemaphoreType.DMA((inner,)),
        ],
        (where, *messages, raw, raw2, slope, slope2, turned, point_back, near_ids),
        1,
        away_in=slabs + 3,
    )
    colour = found[:, :count]
    if split == 2:
        other = lax.ppermute(grad, "view", pairing)
        colour = colour + lax.ppermute(found[:, count:], "view", pairing)
        grad = jnp.where(
            half == 0,
            jnp.concatenate([grad, other], axis=1),
            jnp.concatenate([other, grad], axis=1),
        )
    return (colour[None], grad.reshape(chans, depth, cells))


def solution(mesh):
    in_specs = (P(None, "slab", None), P(), P(), P(), P("view", None), P("view", None, "slab"))
    out_specs = (P("view", None, "slab"), P(None, "slab", None))
    return jax.shard_map(
        on_device, mesh=mesh, in_specs=in_specs, out_specs=out_specs, check_vma=False
    )
```

```python
import functools

import jax
import jax.numpy as jnp
from jax import lax
from jax.experimental import pallas as pl
from jax.experimental.pallas import tpu as pltpu
from jax.sharding import PartitionSpec as P

CX = 32
CY = 32
F32 = jnp.float32
BF16 = jnp.bfloat16
VMEM_LIMIT = 24 * 1024 * 1024
VM = pl.BlockSpec(memory_space=pltpu.VMEM)
SM = pl.BlockSpec(memory_space=pltpu.SMEM)


def rows_of(split):
    if split == 1:
        return CX
    return min(CX, -(-(CX // split + 1) // 4) * 4)


def lane_shift(x, amount, y):
    width = x.shape[-1]
    moved = pltpu.roll(x, (-amount) % width, 1)
    if amount == 1:
        keep = y < CY - 1
    elif amount == -1:
        keep = y > 0
    else:
        lane = lax.broadcasted_iota(jnp.int32, x.shape, 1)
        keep = lane < width - CY if amount > 0 else lane >= CY
    return jnp.where(keep, moved, 0.0)


def thirds(x):
    high = x.astype(BF16)
    rest = x - high.astype(F32)
    mid = rest.astype(BF16)
    low = (rest - mid.astype(F32)).astype(BF16)
    return jnp.concatenate([high, mid, low], axis=0)


def softplus(x):
    return jnp.maximum(x, 0.0) + jnp.log1p(jnp.exp(-jnp.abs(x)))


def swap(x):
    return pltpu.roll(x, 4, 0)


def spread(x, put):
    chans, width = x.shape
    lane = lax.broadcasted_iota(jnp.int32, (chans, width), 1)

    def keep(inside):
        return jnp.where(inside, 1.0, 0.0).astype(BF16)

    before = pltpu.roll(x * keep(lane % CY != CY - 1), 1, 1)
    after = pltpu.roll(x * keep(lane % CY != 0), width - 1, 1)
    for j, by_y in enumerate((before, x, after)):
        put(chans * j, pltpu.roll(by_y * keep(lane < width - CY), CY, 1))
        put(chans * (3 + j), by_y)
        put(chans * (6 + j), pltpu.roll(by_y * keep(lane >= CY), width - CY, 1))


def composed(taps, depth, e):
    total = None
    for a in range(2):
        for b in range(2):
            for c in range(2):
                d = (a + 2 - e[0], b + 2 - e[1], c + 2 - e[2])
                if min(d) >= 0 and max(d) <= 2:
                    at = 9 * d[0] + 3 * d[1] + d[2]
                    term = depth[at : at + 1, :] * taps[4 * a + 2 * b + c]
                    total = term if total is None else total + term
    return total


def near(parity):
    return (-1, 0) if parity == 0 else (0, 1)


def decode_pair(layers, wide_ref, point, slope_ref, raw_ref, k):
    chans = wide_ref.shape[1] // 4
    features = []
    for b in range(2):
        for c in range(2):
            around = jnp.concatenate(
                [
                    layers[j](chans * (3 * (nx + 1) + ny + 1))
                    for j in range(2)
                    for nx in near(b)
                    for ny in near(c)
                ],
                axis=0,
            )
            dw = jnp.dot(wide_ref[2 * b + c], around, preferred_element_type=F32)
            dw = dw[: 2 * chans] + dw[2 * chans :]
            sig = jax.nn.sigmoid(dw)
            silu = dw * sig
            row = 2 * chans * (2 * b + c)
            slope_ref[k, row : row + 2 * chans, :] = silu + sig * (1.0 - silu)
            features.append(silu.astype(BF16))
    raw_ref[k] = jnp.dot(point, jnp.concatenate(features, axis=0), preferred_element_type=F32)


def weight_kernel(
    tconv_ref, depth_ref, weight_ref, wide_ref, turned_ref, point_ref, back_ref,
    taps_ref, depth_pad_ref, full_ref, full2_ref,
):
    chans = tconv_ref.shape[0]
    taps_ref[:, 0:chans] = tconv_ref[...].astype(F32).reshape(8 * chans, chans)
    taps = [taps_ref[pl.ds(q, chans, stride=8), :][:, :chans] for q in range(8)]
    depth_pad_ref[:, 0:27] = depth_ref[...]
    depth = depth_pad_ref[...].T
    for b in range(2):
        for c in range(2):
            for first in range(2):
                for j in range(2):
                    for nx in near(b):
                        for ny in near(c):
                            e = (2 - 2 * j + first, b - 2 * nx + 1, c - 2 * ny + 1)
                            at = chans * (4 * j + 2 * (nx - near(b)[0]) + ny - near(c)[0])
                            col = chans * first
                            full_ref[2 * b + c, at : at + chans, col : col + chans] = composed(taps, depth, e)
            whole = full_ref[2 * b + c].T[: 2 * chans]
            high = whole.astype(BF16)
            wide_ref[2 * b + c, : 2 * chans, :] = high
            wide_ref[2 * b + c, 2 * chans :, :] = (whole - high.astype(F32)).astype(BF16)
    full2_ref[...] = jnp.zeros_like(full2_ref)
    for b in range(2):
        for n in range(2):
            nx = n - b
            for ny in (-1, 0, 1):
                row = chans * (3 * n + ny + 1)
                for j in range(4):
                    for c in range(2):
                        e = (j, 2 * nx + b + 1, 2 * ny + c + 1)
                        if 0 <= e[2] < 4:
                            col = chans * (4 * (j // 2) + 2 * c + j % 2)
                            full2_ref[b, row : row + chans, col : col + chans] = composed(taps, depth, e)
    turned_ref[...] = full2_ref[...].astype(BF16)
    weight = weight_ref[...].astype(F32)
    lines = jnp.concatenate([weight] * 8, axis=1)
    lines = jnp.concatenate([jnp.broadcast_to(lines[o : o + 1], (8, 8 * chans)) for o in range(4)], axis=0)
    row = lax.broadcasted_iota(jnp.int32, lines.shape, 0) % 8
    col = lax.broadcasted_iota(jnp.int32, lines.shape, 1) // chans
    lines = jnp.where(col == 2 * (row % 4) + row // 4, lines, 0.0)
    point_ref[...] = lines.astype(BF16)
    turned = lines.T
    back_ref[...] = jnp.concatenate([turned] * 3, axis=1).astype(BF16)


def pack_kernel(where_ref, window_ref, targets_ref, ids_ref, one_ref, two_ref):
    depth, chans, width = window_ref.shape
    count = targets_ref.shape[2]
    slab = where_ref[0]
    even = lax.rem(slab, 2) == 0
    first, last = window_ref[0].astype(F32), window_ref[depth - 1].astype(F32)
    ids = ids_ref[:, pl.ds(pl.multiple_of(slab * count, 128), count)].astype(F32)
    block = jnp.concatenate([targets_ref[0], targets_ref[1], targets_ref[2], ids], axis=0)
    rows = jnp.concatenate([thirds(block).astype(F32), jnp.zeros((4, count), F32)], axis=0)
    rows = jnp.concatenate([rows, jnp.zeros((16, width - count), F32)], axis=1).astype(BF16)
    one_ref[0:chans, :] = jnp.where(even, last, first).astype(BF16)
    two_ref[0:chans, :] = jnp.where(even, first, last).astype(BF16)
    one_ref[chans : chans + 16, :] = rows
    two_ref[chans : chans + 16, :] = rows


def block_at(ref, j, count):
    x = ref[:, count * j : count * (j + 1)].astype(F32)
    return x[0:4] + x[4:8] + x[8:12]


def inner_kernel(lat_ref, wide_ref, point_ref, away_ref, raw_ref, edge_ref, x9_ref, slope_ref, sems):
    layers, chans, width = lat_ref.shape


    def layer(k):
        def put(at, block):
            x9_ref[k, at : at + chans, :] = block

        spread(lat_ref[k], put)

    layer(0)
    for k in range(layers - 1):
        layer(k + 1)
        around = [lambda at, j=j: x9_ref[k + j, at : at + chans, :] for j in range(2)]
        decode_pair(around, wide_ref, point_ref[...], slope_ref, raw_ref, k)
        pltpu.make_async_copy(slope_ref.at[k], away_ref.at[k], sems.at[k]).start()
    edge_ref[0] = x9_ref[0]
    edge_ref[1] = x9_ref[layers - 1]
    for k in range(layers - 1):
        pltpu.make_async_copy(slope_ref.at[k], away_ref.at[k], sems.at[k]).wait()


def outer_kernel(
    scale, where_ref, one_ref, two_ref, edge_ref, wide_ref, point_ref, inner_ref,
    slope_ref, raw_ref, tot_ref, x9_ref,
):
    slab, slabs = where_ref[0], where_ref[3]
    width = one_ref.shape[1]
    chans = edge_ref.shape[1] // 9
    pairs = inner_ref.shape[0] + 2
    even = lax.rem(slab, 2) == 0
    one, two = one_ref[0:chans, :].astype(F32), two_ref[0:chans, :].astype(F32)
    low = jnp.where(slab == 0, 0.0, jnp.where(even, two, one))
    high = jnp.where(slab == slabs - 1, 0.0, jnp.where(even, one, two))
    for k, x in ((0, low), (1, high)):

        def put(at, block, k=k):
            x9_ref[k, at : at + chans, :] = block

        spread(x.astype(BF16), put)
        layers = [lambda at, k=k: x9_ref[k, at : at + chans, :], lambda at, k=k: edge_ref[k, at : at + chans, :]]
        decode_pair(layers if k == 0 else layers[::-1], wide_ref, point_ref[...], slope_ref, raw_ref, k)
    second = lax.broadcasted_iota(jnp.int32, (8, width), 0) >= 4
    before = jnp.zeros((8, width), F32)
    colour = [jnp.zeros((8, width), F32) for _ in range(3)]
    for k in range(pairs):
        raw = raw_at(raw_ref, inner_ref, k)
        tau = softplus(raw[0:8]) * scale
        if k == 0:
            tau = jnp.where(second, tau, 0.0)
        if k == pairs - 1:
            tau = jnp.where(second, 0.0, tau)
        other = swap(tau)
        weight = jnp.exp(-(before + jnp.where(second, other, 0.0))) * (1.0 - jnp.exp(-tau))
        before = before + (tau + other)
        for o in range(3):
            colour[o] = colour[o] + weight * jax.nn.sigmoid(raw[8 * o + 8 : 8 * o + 16])
    colour = [c + swap(c) for c in colour]
    tot_ref[0:8, :] = jnp.where(second, colour[0], before)
    tot_ref[8:16, :] = jnp.where(second, colour[2], colour[1])


def raw_at(outer_ref, inner_ref, k):
    last = inner_ref.shape[0] + 1
    if k == 0:
        return outer_ref[0]
    if k == last:
        return outer_ref[1]
    return inner_ref[k - 1]


def cell_of(ids):
    fine_x, fine_y = ids // (2 * CY), ids % (2 * CY)
    return (fine_x // 2) * CY + fine_y // 2, (fine_x % 2) * 2 + fine_y % 2


def target_kernel(count, where_ref, tot_ref, *refs):
    *block_refs, msg_ref, near_ref = refs
    width = tot_ref.shape[1]
    start = where_ref[1]
    msg_ref[0:16, :] = tot_ref[...]
    row = lax.broadcasted_iota(jnp.int32, (16, count), 0)
    cells = lax.broadcasted_iota(jnp.int32, (count, width), 1)
    total = jnp.zeros((48, width), F32)
    for i, ref in enumerate(block_refs):
        for j in range(ref.shape[1] // count):
            block = block_at(ref, j, count)
            if j == 0:
                near_ref[:, count * i : count * (i + 1)] = block[3:4, :].astype(jnp.int32)
            cell, part = cell_of(block[3:4, :].astype(jnp.int32))
            value = jnp.where(row < 4, 1.0, jnp.where(row < 8, block[0:1, :], jnp.where(row < 12, block[1:2, :], block[2:3, :])))
            value = jnp.where(row % 4 == part, value, 0.0)
            column = jnp.broadcast_to(cell - start, (8, count)).astype(F32).T[:, 0:1].astype(jnp.int32)
            hot = jnp.where(cells == column, 1.0, 0.0).astype(BF16)
            total = total + jnp.dot(thirds(value), hot, preferred_element_type=F32)
    msg_ref[16:32, :] = total[0:16] + (total[16:32] + total[32:48])


def back_kernel(scale, where_ref, *refs):
    (*msg_refs, inner_ref, outer_ref, away_ref, slope2_ref, wide_ref, point_ref, near_ref) = refs[:-8]
    grad_ref, colour_ref, gdw_ref, e_ref, w_ref, tile_ref, slope_ref, sems = refs[-8:]
    slab, start, own_start = where_ref[0], where_ref[1], where_ref[2]
    slabs = len(msg_refs)
    inner, _, width = inner_ref.shape
    pairs = inner + 2
    chans = slope_ref.shape[1] // 8
    own_width = grad_ref.shape[1]
    second = lax.broadcasted_iota(jnp.int32, (8, width), 0) >= 4
    loads = [pltpu.make_async_copy(away_ref.at[k], slope_ref.at[k], sems.at[k]) for k in range(inner)]
    for load in loads:
        load.start()

    def both(x):
        other = swap(x)
        return jnp.where(second, other, x), jnp.where(second, x, other)

    totals, colours, hits = [], [], None
    for ref in msg_refs:
        tau_total, c0 = both(ref[0:8, :])
        c1, c2 = both(ref[8:16, :])
        totals.append(tau_total)
        colours.append((c0, c1, c2))
        here = (ref[16:24, :], ref[24:32, :])
        hits = here if hits is None else (hits[0] + here[0], hits[1] + here[1])
    index = [lax.rem(slab - k + slabs, slabs) for k in range(slabs)]
    full = [jnp.zeros((8, width), F32) for _ in range(3)]
    after = [jnp.zeros((8, width), F32) for _ in range(3)]
    prefix = None
    for k in range(slabs):
        ahead = jnp.zeros((8, width), F32)
        for other in range(slabs):
            if other != k:
                ahead = ahead + jnp.where(index[other] < index[k], totals[other], 0.0)
        if k == 0:
            prefix = ahead
        through = jnp.exp(-ahead)
        for o in range(3):
            part = through * colours[k][o]
            full[o] = full[o] + part
            if k:
                after[o] = after[o] + jnp.where(index[k] > slab, part, 0.0)
    number, t0 = both(hits[0])
    t1, t2 = both(hits[1])
    pull = [number * full[o] - t for o, t in enumerate((t0, t1, t2))]

    tau0 = softplus(outer_ref[0, 0:8, :]) * scale
    before = -both(tau0)[0]
    for k in range(pairs):
        tau = softplus(raw_at(outer_ref, inner_ref, k)[0:8]) * scale
        other = swap(tau)
        through = jnp.exp(-(prefix + (before + jnp.where(second, other, 0.0))))
        before = before + (tau + other)
        left = jnp.exp(-tau)
        w_ref[k, 0:8, :] = through * (1.0 - left)
        w_ref[k, 8:16, :] = through * left
    last = pairs - 1
    for o in range(3):
        e = w_ref[last, 0:8, :] * jax.nn.sigmoid(outer_ref[1, 8 * o + 8 : 8 * o + 16, :])
        after[o] = after[o] - both(e)[1]
    for k in range(pairs - 1, -1, -1):
        weight, later = w_ref[k, 0:8, :], w_ref[k, 8:16, :]
        raw = raw_at(outer_ref, inner_ref, k)
        total = jnp.zeros((8, width), F32)
        outside = None
        if k == 0:
            outside = jnp.logical_and(jnp.logical_not(second), slab == 0)
        if k == last:
            outside = jnp.logical_and(second, slab == slabs - 1)
        for o in range(3):
            rgb = jax.nn.sigmoid(raw[8 * o + 8 : 8 * o + 16])
            e = weight * rgb
            other = swap(e)
            rest = after[o] + jnp.where(second, 0.0, other)
            after[o] = after[o] + (e + other)
            total = total + pull[o] * (later * rgb - rest)
            grad = pull[o] * (e * (1.0 - rgb))
            if outside is not None:
                grad = jnp.where(outside, 0.0, grad)
            e_ref[k, 8 * o + 8 : 8 * o + 16, :] = grad
        grad = total * (scale * jax.nn.sigmoid(raw[0:8]))
        if outside is not None:
            grad = jnp.where(outside, 0.0, grad)
        e_ref[k, 0:8, :] = grad

    count = near_ref.shape[1]
    cell, part = cell_of(near_ref[...])
    cell = cell - own_start
    mine = jnp.logical_and(cell >= 0, cell < own_width)
    cell = jnp.where(mine, cell + (own_start - start), -1)
    hot = jnp.where(lax.broadcasted_iota(jnp.int32, (width, count), 0) == cell, 1.0, 0.0).astype(BF16)
    rows = jnp.concatenate(
        [jnp.where(second, full[1], full[0]), jnp.where(second, full[2], full[2])], axis=0
    )
    found = jnp.dot(thirds(rows), hot, preferred_element_type=F32)
    found = found[0:16] + (found[16:32] + found[32:48])
    row = lax.broadcasted_iota(jnp.int32, (16, count), 0)
    found = jnp.where(row % 4 == part, found, 0.0)
    for o in range(3):
        colour_ref[o : o + 1, :] = jnp.sum(found[4 * o : 4 * o + 4], axis=0, keepdims=True)

    def pair(k):
        if 0 < k < last:
            loads[k - 1].wait()
        slope = slope_ref[k - 1] if 0 < k < last else slope2_ref[k // last]
        grad_features = jnp.dot(point_ref[...], thirds(e_ref[k]), preferred_element_type=F32)
        gdw_ref[k] = (grad_features * slope).astype(BF16)

    y = lax.broadcasted_iota(jnp.int32, (chans, width), 1) % CY
    low = own_start == start
    for k in (0, last, *range(1, last)):
        pair(k)
    for z in range(pairs - 1):
        every = []
        for b in range(2):
            at = 4 * chans * b
            around = gdw_ref[z : z + 2, at : at + 4 * chans, :].reshape(8 * chans, width)
            every.append(jnp.dot(wide_ref[b], around, preferred_element_type=F32))
        total = None
        for j in range(3):
            at = chans * j
            line = every[0][at : at + chans] + every[1][at + 3 * chans : at + 4 * chans]
            line = line + lane_shift(every[1][at : at + chans], -CY, y)
            line = line + lane_shift(every[0][at + 3 * chans : at + 4 * chans], CY, y)
            if j != 1:
                line = lane_shift(line, j - 1, y)
            total = line if total is None else total + line
        if own_width < width:
            total = jnp.where(low, total[:, :own_width], total[:, width - own_width :])
        for t in range(own_width // 128):
            tile_ref[t, pl.ds(z, chans, stride=pairs - 1), :] = total[:, 128 * t : 128 * t + 128]
    for t in range(own_width // 128):
        grad_ref[:, 128 * t : 128 * t + 128] = tile_ref[t]


def call(kernel, outs, scratch, operands, smem, far=(), away=(), away_out=None):
    operands = list(operands)
    specs = [SM] * smem + [VM] * (len(operands) - smem)
    out_specs = [VM] * len(outs)
    shapes = [jax.ShapeDtypeStruct(s, t) for s, t in outs]
    for i in far:
        operands[i] = pltpu.with_memory_space_constraint(operands[i], pltpu.HBM)
    for i in away:
        specs[i] = pl.BlockSpec(memory_space=pltpu.HBM)
    if away_out is not None:
        shapes[away_out] = pltpu.HBM(*outs[away_out])
        out_specs[away_out] = pl.BlockSpec(memory_space=pltpu.HBM)
    return pl.pallas_call(
        kernel,
        out_shape=shapes,
        in_specs=specs,
        out_specs=out_specs,
        scratch_shapes=[pltpu.VMEM(*x) if isinstance(x, tuple) else x for x in scratch],
        compiler_params=pltpu.CompilerParams(vmem_limit_bytes=VMEM_LIMIT),
    )(*operands)


def on_device(latent, tconv_weight, depth_weight, point_weight, pencil_ids, targets):
    chans, depth, cells = latent.shape
    view, slab = lax.axis_index("view"), lax.axis_index("slab")
    views, slabs = lax.axis_size("view"), lax.axis_size("slab")
    count = targets.shape[2]
    split = 2 if views % 2 == 0 else 1
    rows = rows_of(split)
    width, own_width = rows * CY, cells // split
    half = view % split
    start = half * (cells - width)
    own_start = half * own_width
    where = jnp.stack([slab, start, own_start, slabs]).astype(jnp.int32)
    scale = 1.5 / (2 * depth * slabs)

    window = lax.dynamic_slice_in_dim(jnp.transpose(latent, (1, 0, 2)), start, width, axis=2)
    one, two = call(
        pack_kernel,
        [((chans + 16, width), BF16)] * 2,
        [],
        (where, window, jnp.transpose(targets, (1, 0, 2)), pencil_ids),
        1,
        far=(2, 3),
    )

    def send(x, mask, partner):
        pairs = [(v * slabs + s, (v ^ mask) * slabs + partner(s)) for v in range(views) for s in range(slabs)]
        return lax.ppermute(x, ("view", "slab"), pairs)

    wide, turned, point, point_back = call(
        weight_kernel,
        [
            ((4, 4 * chans, 8 * chans), BF16),
            ((2, 6 * chans, 8 * chans), BF16),
            ((32, 8 * chans), BF16),
            ((8 * chans, 96), BF16),
        ],
        [((8 * chans, 128), F32), ((chans, 128), F32), ((4, 8 * chans, 128), F32), ((2, 6 * chans, 8 * chans), F32)],
        (jnp.transpose(tconv_weight, (0, 2, 1)), depth_weight, point_weight),
        0,
        far=(0, 1, 2),
    )

    masks = [split << k for k in range((views // split).bit_length() - 1)]
    blocks = two[chans:, :count]
    one = send(one, masks[0] if masks else 0, lambda s: (s + 1 - 2 * (s % 2)) % slabs)
    one, wide = lax.optimization_barrier((one, wide))
    if masks:
        two = lax.dynamic_update_slice(two, one[chans:, :count], (chans, count))
        blocks = two[chans:, : 2 * count]
    two = send(two, masks[1] if len(masks) > 1 else 0, lambda s: (s + 2 * (s % 2) - 1) % slabs)
    inner = depth - 1
    slope, raw, edge = call(
        inner_kernel,
        [((inner, 8 * chans, width), F32), ((inner, 32, width), F32), ((2, 9 * chans, width), BF16)],
        [
            ((depth, 9 * chans, width), BF16),
            ((inner, 8 * chans, width), F32),
            pltpu.SemaphoreType.DMA((inner,)),
        ],
        (window, wide, point),
        0,
        away_out=0,
    )
    two, raw, edge = lax.optimization_barrier((two, raw, edge))
    if len(masks) > 1:
        blocks = jnp.concatenate([blocks, two[chans:, : 2 * count]], axis=1)
    for mask in masks[2:]:
        blocks = jnp.concatenate([blocks, send(blocks, mask, lambda s: s)], axis=1)
    groups = [blocks]
    if split == 2:
        pairing = [(i, i ^ 1) for i in range(views)]
        groups.append(lax.ppermute(blocks, "view", pairing))
    slope2, raw2, tot = call(
        functools.partial(outer_kernel, scale),
        [((2, 8 * chans, width), F32), ((2, 32, width), F32), ((16, width), F32)],
        [((2, 9 * chans, width), BF16)],
        (where, one, two, edge, wide, point, raw),
        1,
    )
    message, near_ids = call(
        functools.partial(target_kernel, count),
        [((32, width), F32), ((1, split * count), jnp.int32)],
        [],
        (where, tot, *groups),
        1,
    )
    messages = [message]
    for k in range(1, slabs):
        messages.append(lax.ppermute(message, "slab", [(i, (i + k) % slabs) for i in range(slabs)]))
    grad, found = call(
        functools.partial(back_kernel, scale),
        [((chans * depth, own_width), F32), ((3, split * count), F32)],
        [
            ((inner + 2, 8 * chans, width), BF16),
            ((inner + 2, 32, width), F32),
            ((inner + 2, 16, width), F32),
            ((own_width // 128, chans * depth, 128), F32),
            ((inner, 8 * chans, width), F32),
            pltpu.SemaphoreType.DMA((inner,)),
        ],
        (where, *messages, raw, raw2, slope, slope2, turned, point_back, near_ids),
        1,
        far=(slabs + 3,),
        away=(slabs + 3,),
    )
    colour = found[:, :count]
    if split == 2:
        other = lax.ppermute(grad, "view", pairing)
        colour = colour + lax.ppermute(found[:, count:], "view", pairing)
        grad = jnp.where(
            half == 0,
            jnp.concatenate([grad, other], axis=1),
            jnp.concatenate([other, grad], axis=1),
        )
    return (colour[None], grad.reshape(chans, depth, cells))


def solution(mesh):
    in_specs = (P(None, "slab", None), P(), P(), P(), P("view", None), P("view", None, "slab"))
    out_specs = (P("view", None, "slab"), P(None, "slab", None))
    return jax.shard_map(
        on_device, mesh=mesh, in_specs=in_specs, out_specs=out_specs, check_vma=False
    )
```

```python
import functools

import jax
import jax.numpy as jnp
from jax import lax
from jax.experimental import pallas as pl
from jax.experimental.pallas import tpu as pltpu
from jax.sharding import PartitionSpec as P

CX = 32
CY = 32
F32 = jnp.float32
BF16 = jnp.bfloat16
VMEM_LIMIT = 24 * 1024 * 1024
VM = pl.BlockSpec(memory_space=pltpu.VMEM)
SM = pl.BlockSpec(memory_space=pltpu.SMEM)


def rows_of(split):
    if split == 1:
        return CX
    return min(CX, -(-(CX // split + 1) // 4) * 4)


def lane_shift(x, amount, y):
    width = x.shape[-1]
    moved = pltpu.roll(x, (-amount) % width, 1)
    if amount == 1:
        keep = y < CY - 1
    elif amount == -1:
        keep = y > 0
    else:
        lane = lax.broadcasted_iota(jnp.int32, x.shape, 1)
        keep = lane < width - CY if amount > 0 else lane >= CY
    return jnp.where(keep, moved, 0.0)


def thirds(x):
    high = x.astype(BF16)
    rest = x - high.astype(F32)
    mid = rest.astype(BF16)
    low = (rest - mid.astype(F32)).astype(BF16)
    return jnp.concatenate([high, mid, low], axis=0)


def softplus(x):
    return jnp.maximum(x, 0.0) + jnp.log1p(jnp.exp(-jnp.abs(x)))


def partner(slab, k, slabs):
    if slabs & (slabs - 1) == 0:
        return slab ^ k
    return (slab - k + slabs) % slabs


def swap(x):
    return pltpu.roll(x, 4, 0)


def spread(x, put):
    chans, width = x.shape
    lane = lax.broadcasted_iota(jnp.int32, (chans, width), 1)

    def keep(inside):
        return jnp.where(inside, 1.0, 0.0).astype(BF16)

    before = pltpu.roll(x * keep(lane % CY != CY - 1), 1, 1)
    after = pltpu.roll(x * keep(lane % CY != 0), width - 1, 1)
    for j, by_y in enumerate((before, x, after)):
        put(chans * j, pltpu.roll(by_y * keep(lane < width - CY), CY, 1))
        put(chans * (3 + j), by_y)
        put(chans * (6 + j), pltpu.roll(by_y * keep(lane >= CY), width - CY, 1))


def composed(taps, depth, e):
    total = None
    for a in range(2):
        for b in range(2):
            for c in range(2):
                d = (a + 2 - e[0], b + 2 - e[1], c + 2 - e[2])
                if min(d) >= 0 and max(d) <= 2:
                    at = 9 * d[0] + 3 * d[1] + d[2]
                    term = depth[at : at + 1, :] * taps[4 * a + 2 * b + c]
                    total = term if total is None else total + term
    return total


def near(parity):
    return (-1, 0) if parity == 0 else (0, 1)


def decode_pair(layers, wide_ref, point, slope_ref, raw_ref, k):
    chans = wide_ref.shape[1] // 4
    features = []
    for b in range(2):
        for c in range(2):
            around = jnp.concatenate(
                [
                    layers[j](chans * (3 * (nx + 1) + ny + 1))
                    for j in range(2)
                    for nx in near(b)
                    for ny in near(c)
                ],
                axis=0,
            )
            dw = jnp.dot(wide_ref[2 * b + c], around, preferred_element_type=F32)
            dw = dw[: 2 * chans] + dw[2 * chans :]
            sig = jax.nn.sigmoid(dw)
            silu = dw * sig
            row = 2 * chans * (2 * b + c)
            slope_ref[k, row : row + 2 * chans, :] = silu + sig * (1.0 - silu)
            features.append(silu.astype(BF16))
    raw_ref[k] = jnp.dot(point, jnp.concatenate(features, axis=0), preferred_element_type=F32)


def weight_kernel(
    tconv_ref, depth_ref, weight_ref, wide_ref, turned_ref, point_ref, back_ref,
    taps_ref, depth_pad_ref, full_ref, full2_ref,
):
    chans = tconv_ref.shape[0]
    taps_ref[:, 0:chans] = tconv_ref[...].astype(F32).reshape(8 * chans, chans)
    taps = [taps_ref[pl.ds(q, chans, stride=8), :][:, :chans] for q in range(8)]
    depth_pad_ref[:, 0:27] = depth_ref[...]
    depth = depth_pad_ref[...].T
    for b in range(2):
        for c in range(2):
            for first in range(2):
                for j in range(2):
                    for nx in near(b):
                        for ny in near(c):
                            e = (2 - 2 * j + first, b - 2 * nx + 1, c - 2 * ny + 1)
                            at = chans * (4 * j + 2 * (nx - near(b)[0]) + ny - near(c)[0])
                            col = chans * first
                            full_ref[2 * b + c, at : at + chans, col : col + chans] = composed(taps, depth, e)
            whole = full_ref[2 * b + c].T[: 2 * chans]
            high = whole.astype(BF16)
            wide_ref[2 * b + c, : 2 * chans, :] = high
            wide_ref[2 * b + c, 2 * chans :, :] = (whole - high.astype(F32)).astype(BF16)
    full2_ref[...] = jnp.zeros_like(full2_ref)
    for b in range(2):
        for n in range(2):
            nx = n - b
            for ny in (-1, 0, 1):
                row = chans * (3 * n + ny + 1)
                for j in range(4):
                    for c in range(2):
                        e = (j, 2 * nx + b + 1, 2 * ny + c + 1)
                        if 0 <= e[2] < 4:
                            col = chans * (4 * (j // 2) + 2 * c + j % 2)
                            full2_ref[b, row : row + chans, col : col + chans] = composed(taps, depth, e)
    turned_ref[...] = full2_ref[...].astype(BF16)
    weight = weight_ref[...].astype(F32)
    lines = jnp.concatenate([weight] * 8, axis=1)
    lines = jnp.concatenate([jnp.broadcast_to(lines[o : o + 1], (8, 8 * chans)) for o in range(4)], axis=0)
    row = lax.broadcasted_iota(jnp.int32, lines.shape, 0) % 8
    col = lax.broadcasted_iota(jnp.int32, lines.shape, 1) // chans
    lines = jnp.where(col == 2 * (row % 4) + row // 4, lines, 0.0)
    point_ref[...] = lines.astype(BF16)
    turned = lines.T
    back_ref[...] = jnp.concatenate([turned] * 3, axis=1).astype(BF16)


def pack_kernel(where_ref, window_ref, targets_ref, ids_ref, one_ref, two_ref):
    depth, chans, width = window_ref.shape
    count = targets_ref.shape[2]
    slab = where_ref[0]
    even = lax.rem(slab, 2) == 0
    first, last = window_ref[0].astype(F32), window_ref[depth - 1].astype(F32)
    ids = ids_ref[:, pl.ds(pl.multiple_of(slab * count, 128), count)].astype(F32)
    block = jnp.concatenate([targets_ref[0], targets_ref[1], targets_ref[2], ids], axis=0)
    rows = jnp.concatenate([thirds(block).astype(F32), jnp.zeros((4, count), F32)], axis=0)
    rows = jnp.concatenate([rows, jnp.zeros((16, width - count), F32)], axis=1).astype(BF16)
    one_ref[0:chans, :] = jnp.where(even, last, first).astype(BF16)
    two_ref[0:chans, :] = jnp.where(even, first, last).astype(BF16)
    one_ref[chans : chans + 16, :] = rows
    two_ref[chans : chans + 16, :] = rows


def block_at(ref, j, count):
    x = ref[:, count * j : count * (j + 1)].astype(F32)
    return x[0:4] + x[4:8] + x[8:12]


def inner_kernel(lat_ref, wide_ref, point_ref, away_ref, raw_ref, edge_ref, x9_ref, slope_ref, sems):
    layers, chans, width = lat_ref.shape


    def layer(k):
        def put(at, block):
            x9_ref[k, at : at + chans, :] = block

        spread(lat_ref[k], put)

    layer(0)
    for k in range(layers - 1):
        layer(k + 1)
        around = [lambda at, j=j: x9_ref[k + j, at : at + chans, :] for j in range(2)]
        decode_pair(around, wide_ref, point_ref[...], slope_ref, raw_ref, k)
        pltpu.make_async_copy(slope_ref.at[k], away_ref.at[k], sems.at[k]).start()
    edge_ref[0] = x9_ref[0]
    edge_ref[1] = x9_ref[layers - 1]
    for k in range(layers - 1):
        pltpu.make_async_copy(slope_ref.at[k], away_ref.at[k], sems.at[k]).wait()


def outer_kernel(
    scale, where_ref, one_ref, two_ref, edge_ref, wide_ref, point_ref, inner_ref,
    slope_ref, raw_ref, tot_ref, x9_ref,
):
    slab, slabs = where_ref[0], where_ref[3]
    width = one_ref.shape[1]
    chans = edge_ref.shape[1] // 9
    pairs = inner_ref.shape[0] + 2
    even = lax.rem(slab, 2) == 0
    one, two = one_ref[0:chans, :].astype(F32), two_ref[0:chans, :].astype(F32)
    low = jnp.where(slab == 0, 0.0, jnp.where(even, two, one))
    high = jnp.where(slab == slabs - 1, 0.0, jnp.where(even, one, two))
    for k, x in ((0, low), (1, high)):

        def put(at, block, k=k):
            x9_ref[k, at : at + chans, :] = block

        spread(x.astype(BF16), put)
        layers = [lambda at, k=k: x9_ref[k, at : at + chans, :], lambda at, k=k: edge_ref[k, at : at + chans, :]]
        decode_pair(layers if k == 0 else layers[::-1], wide_ref, point_ref[...], slope_ref, raw_ref, k)
    second = lax.broadcasted_iota(jnp.int32, (8, width), 0) >= 4
    before = jnp.zeros((8, width), F32)
    colour = [jnp.zeros((8, width), F32) for _ in range(3)]
    for k in range(pairs):
        raw = raw_at(raw_ref, inner_ref, k)
        tau = softplus(raw[0:8]) * scale
        if k == 0:
            tau = jnp.where(second, tau, 0.0)
        if k == pairs - 1:
            tau = jnp.where(second, 0.0, tau)
        other = swap(tau)
        weight = jnp.exp(-(before + jnp.where(second, other, 0.0))) * (1.0 - jnp.exp(-tau))
        before = before + (tau + other)
        for o in range(3):
            colour[o] = colour[o] + weight * jax.nn.sigmoid(raw[8 * o + 8 : 8 * o + 16])
    colour = [c + swap(c) for c in colour]
    tot_ref[0:8, :] = jnp.where(second, colour[0], before)
    tot_ref[8:16, :] = jnp.where(second, colour[2], colour[1])


def raw_at(outer_ref, inner_ref, k):
    last = inner_ref.shape[0] + 1
    if k == 0:
        return outer_ref[0]
    if k == last:
        return outer_ref[1]
    return inner_ref[k - 1]


def cell_of(ids):
    fine_x, fine_y = ids // (2 * CY), ids % (2 * CY)
    return (fine_x // 2) * CY + fine_y // 2, (fine_x % 2) * 2 + fine_y % 2


def target_kernel(count, where_ref, tot_ref, *refs):
    *block_refs, msg_ref, near_ref = refs
    width = tot_ref.shape[1]
    start = where_ref[1]
    msg_ref[0:16, :] = tot_ref[...]
    row = lax.broadcasted_iota(jnp.int32, (16, count), 0)
    cells = lax.broadcasted_iota(jnp.int32, (count, width), 1)
    total = jnp.zeros((48, width), F32)
    for i, ref in enumerate(block_refs):
        for j in range(ref.shape[1] // count):
            block = block_at(ref, j, count)
            if j == 0:
                near_ref[:, count * i : count * (i + 1)] = block[3:4, :].astype(jnp.int32)
            cell, part = cell_of(block[3:4, :].astype(jnp.int32))
            value = jnp.where(row < 4, 1.0, jnp.where(row < 8, block[0:1, :], jnp.where(row < 12, block[1:2, :], block[2:3, :])))
            value = jnp.where(row % 4 == part, value, 0.0)
            column = jnp.broadcast_to(cell - start, (8, count)).astype(F32).T[:, 0:1].astype(jnp.int32)
            hot = jnp.where(cells == column, 1.0, 0.0).astype(BF16)
            total = total + jnp.dot(thirds(value), hot, preferred_element_type=F32)
    msg_ref[16:32, :] = total[0:16] + (total[16:32] + total[32:48])


def back_kernel(scale, where_ref, *refs):
    (*msg_refs, inner_ref, outer_ref, away_ref, slope2_ref, wide_ref, point_ref, near_ref) = refs[:-8]
    grad_ref, colour_ref, gdw_ref, e_ref, w_ref, tile_ref, slope_ref, sems = refs[-8:]
    slab, start, own_start = where_ref[0], where_ref[1], where_ref[2]
    slabs = len(msg_refs)
    inner, _, width = inner_ref.shape
    pairs = inner + 2
    chans = slope_ref.shape[1] // 8
    own_width = grad_ref.shape[1]
    second = lax.broadcasted_iota(jnp.int32, (8, width), 0) >= 4
    cuts = (0, inner // 3, 2 * inner // 3, inner)
    loads = [
        pltpu.make_async_copy(away_ref.at[a:b], slope_ref.at[a:b], sems.at[i])
        for i, (a, b) in enumerate(zip(cuts, cuts[1:]))
    ]
    for load in loads:
        load.start()

    def both(x):
        other = swap(x)
        return jnp.where(second, other, x), jnp.where(second, x, other)

    totals, colours, hits = [], [], None
    for ref in msg_refs:
        tau_total, c0 = both(ref[0:8, :])
        c1, c2 = both(ref[8:16, :])
        totals.append(tau_total)
        colours.append((c0, c1, c2))
        here = (ref[16:24, :], ref[24:32, :])
        hits = here if hits is None else (hits[0] + here[0], hits[1] + here[1])
    index = [partner(slab, k, slabs) for k in range(slabs)]
    full = [jnp.zeros((8, width), F32) for _ in range(3)]
    after = [jnp.zeros((8, width), F32) for _ in range(3)]
    prefix = None
    for k in range(slabs):
        ahead = jnp.zeros((8, width), F32)
        for other in range(slabs):
            if other != k:
                ahead = ahead + jnp.where(index[other] < index[k], totals[other], 0.0)
        if k == 0:
            prefix = ahead
        through = jnp.exp(-ahead)
        for o in range(3):
            part = through * colours[k][o]
            full[o] = full[o] + part
            if k:
                after[o] = after[o] + jnp.where(index[k] > slab, part, 0.0)
    number, t0 = both(hits[0])
    t1, t2 = both(hits[1])
    pull = [number * full[o] - t for o, t in enumerate((t0, t1, t2))]

    tau0 = softplus(outer_ref[0, 0:8, :]) * scale
    before = -both(tau0)[0]
    for k in range(pairs):
        tau = softplus(raw_at(outer_ref, inner_ref, k)[0:8]) * scale
        other = swap(tau)
        through = jnp.exp(-(prefix + (before + jnp.where(second, other, 0.0))))
        before = before + (tau + other)
        left = jnp.exp(-tau)
        w_ref[k, 0:8, :] = through * (1.0 - left)
        w_ref[k, 8:16, :] = through * left
    last = pairs - 1
    for o in range(3):
        e = w_ref[last, 0:8, :] * jax.nn.sigmoid(outer_ref[1, 8 * o + 8 : 8 * o + 16, :])
        after[o] = after[o] - both(e)[1]
    for k in range(pairs - 1, -1, -1):
        weight, later = w_ref[k, 0:8, :], w_ref[k, 8:16, :]
        raw = raw_at(outer_ref, inner_ref, k)
        total = jnp.zeros((8, width), F32)
        outside = None
        if k == 0:
            outside = jnp.logical_and(jnp.logical_not(second), slab == 0)
        if k == last:
            outside = jnp.logical_and(second, slab == slabs - 1)
        for o in range(3):
            rgb = jax.nn.sigmoid(raw[8 * o + 8 : 8 * o + 16])
            e = weight * rgb
            other = swap(e)
            rest = after[o] + jnp.where(second, 0.0, other)
            after[o] = after[o] + (e + other)
            total = total + pull[o] * (later * rgb - rest)
            grad = pull[o] * (e * (1.0 - rgb))
            if outside is not None:
                grad = jnp.where(outside, 0.0, grad)
            e_ref[k, 8 * o + 8 : 8 * o + 16, :] = grad
        grad = total * (scale * jax.nn.sigmoid(raw[0:8]))
        if outside is not None:
            grad = jnp.where(outside, 0.0, grad)
        e_ref[k, 0:8, :] = grad

    count = near_ref.shape[1]
    cell, part = cell_of(near_ref[...])
    cell = cell - own_start
    mine = jnp.logical_and(cell >= 0, cell < own_width)
    cell = jnp.where(mine, cell + (own_start - start), -1)
    hot = jnp.where(lax.broadcasted_iota(jnp.int32, (width, count), 0) == cell, 1.0, 0.0).astype(BF16)
    rows = jnp.concatenate(
        [jnp.where(second, full[1], full[0]), jnp.where(second, full[2], full[2])], axis=0
    )
    found = jnp.dot(thirds(rows), hot, preferred_element_type=F32)
    found = found[0:16] + (found[16:32] + found[32:48])
    row = lax.broadcasted_iota(jnp.int32, (16, count), 0)
    found = jnp.where(row % 4 == part, found, 0.0)
    for o in range(3):
        colour_ref[o : o + 1, :] = jnp.sum(found[4 * o : 4 * o + 4], axis=0, keepdims=True)

    def pair(k):
        if k - 1 in cuts[:-1]:
            loads[cuts.index(k - 1)].wait()
        slope = slope_ref[k - 1] if 0 < k < last else slope2_ref[k // last]
        grad_features = jnp.dot(point_ref[...], thirds(e_ref[k]), preferred_element_type=F32)
        gdw_ref[k] = (grad_features * slope).astype(BF16)

    y = lax.broadcasted_iota(jnp.int32, (chans, width), 1) % CY
    low = own_start == start
    for k in (0, last, *range(1, last)):
        pair(k)
    for z in range(pairs - 1):
        every = []
        for b in range(2):
            at = 4 * chans * b
            around = gdw_ref[z : z + 2, at : at + 4 * chans, :].reshape(8 * chans, width)
            every.append(jnp.dot(wide_ref[b], around, preferred_element_type=F32))
        total = None
        for j in range(3):
            at = chans * j
            line = every[0][at : at + chans] + every[1][at + 3 * chans : at + 4 * chans]
            line = line + lane_shift(every[1][at : at + chans], -CY, y)
            line = line + lane_shift(every[0][at + 3 * chans : at + 4 * chans], CY, y)
            if j != 1:
                line = lane_shift(line, j - 1, y)
            total = line if total is None else total + line
        if own_width < width:
            total = jnp.where(low, total[:, :own_width], total[:, width - own_width :])
        for t in range(own_width // 128):
            tile_ref[t, pl.ds(z, chans, stride=pairs - 1), :] = total[:, 128 * t : 128 * t + 128]
    for t in range(own_width // 128):
        grad_ref[:, 128 * t : 128 * t + 128] = tile_ref[t]


def call(kernel, outs, scratch, operands, smem, far=(), away=(), away_out=None):
    operands = list(operands)
    specs = [SM] * smem + [VM] * (len(operands) - smem)
    out_specs = [VM] * len(outs)
    shapes = [jax.ShapeDtypeStruct(s, t) for s, t in outs]
    for i in far:
        operands[i] = pltpu.with_memory_space_constraint(operands[i], pltpu.HBM)
    for i in away:
        specs[i] = pl.BlockSpec(memory_space=pltpu.HBM)
    if away_out is not None:
        shapes[away_out] = pltpu.HBM(*outs[away_out])
        out_specs[away_out] = pl.BlockSpec(memory_space=pltpu.HBM)
    return pl.pallas_call(
        kernel,
        out_shape=shapes,
        in_specs=specs,
        out_specs=out_specs,
        scratch_shapes=[pltpu.VMEM(*x) if isinstance(x, tuple) else x for x in scratch],
        compiler_params=pltpu.CompilerParams(vmem_limit_bytes=VMEM_LIMIT),
    )(*operands)


def on_device(latent, tconv_weight, depth_weight, point_weight, pencil_ids, targets):
    chans, depth, cells = latent.shape
    view, slab = lax.axis_index("view"), lax.axis_index("slab")
    views, slabs = lax.axis_size("view"), lax.axis_size("slab")
    count = targets.shape[2]
    split = 2 if views % 2 == 0 else 1
    rows = rows_of(split)
    width, own_width = rows * CY, cells // split
    half = view % split
    start = half * (cells - width)
    own_start = half * own_width
    where = jnp.stack([slab, start, own_start, slabs]).astype(jnp.int32)
    scale = 1.5 / (2 * depth * slabs)

    window = lax.dynamic_slice_in_dim(jnp.transpose(latent, (1, 0, 2)), start, width, axis=2)
    one, two = call(
        pack_kernel,
        [((chans + 16, width), BF16)] * 2,
        [],
        (where, window, jnp.transpose(targets, (1, 0, 2)), pencil_ids),
        1,
        far=(2, 3),
    )

    def send(x, mask, partner):
        pairs = [(v * slabs + s, (v ^ mask) * slabs + partner(s)) for v in range(views) for s in range(slabs)]
        return lax.ppermute(x, ("view", "slab"), pairs)

    wide, turned, point, point_back = call(
        weight_kernel,
        [
            ((4, 4 * chans, 8 * chans), BF16),
            ((2, 6 * chans, 8 * chans), BF16),
            ((32, 8 * chans), BF16),
            ((8 * chans, 96), BF16),
        ],
        [((8 * chans, 128), F32), ((chans, 128), F32), ((4, 8 * chans, 128), F32), ((2, 6 * chans, 8 * chans), F32)],
        (jnp.transpose(tconv_weight, (0, 2, 1)), depth_weight, point_weight),
        0,
        far=(0, 1, 2),
    )

    chips = views // split
    blocks = [one[chans:, :count]]
    one = send(one, split if chips > 1 else 0, lambda s: (s + 1 - 2 * (s % 2)) % slabs)
    two = send(two, 2 * split if chips > 2 else 0, lambda s: (s + 2 * (s % 2) - 1) % slabs)
    rest = [send(blocks[0], m * split, lambda s: s) for m in range(3, chips)]
    inner = depth - 1
    slope, raw, edge = call(
        inner_kernel,
        [((inner, 8 * chans, width), F32), ((inner, 32, width), F32), ((2, 9 * chans, width), BF16)],
        [
            ((depth, 9 * chans, width), BF16),
            ((inner, 8 * chans, width), F32),
            pltpu.SemaphoreType.DMA((inner,)),
        ],
        (window, wide, point),
        0,
        away_out=0,
    )
    one, two, rest, raw, edge = lax.optimization_barrier((one, two, rest, raw, edge))
    blocks += [one[chans:, :count], two[chans:, :count]][: chips - 1]
    blocks = jnp.concatenate(blocks + rest, axis=1)
    groups = [blocks]
    if split == 2:
        pairing = [(i, i ^ 1) for i in range(views)]
        groups.append(lax.ppermute(blocks, "view", pairing))
    slope2, raw2, tot = call(
        functools.partial(outer_kernel, scale),
        [((2, 8 * chans, width), F32), ((2, 32, width), F32), ((16, width), F32)],
        [((2, 9 * chans, width), BF16)],
        (where, one, two, edge, wide, point, raw),
        1,
    )
    message, near_ids = call(
        functools.partial(target_kernel, count),
        [((32, width), F32), ((1, split * count), jnp.int32)],
        [],
        (where, tot, *groups),
        1,
    )
    messages = [message]
    for k in range(1, slabs):
        messages.append(lax.ppermute(message, "slab", [(partner(i, k, slabs), i) for i in range(slabs)]))
    grad, found = call(
        functools.partial(back_kernel, scale),
        [((chans * depth, own_width), F32), ((3, split * count), F32)],
        [
            ((inner + 2, 8 * chans, width), BF16),
            ((inner + 2, 32, width), F32),
            ((inner + 2, 16, width), F32),
            ((own_width // 128, chans * depth, 128), F32),
            ((inner, 8 * chans, width), F32),
            pltpu.SemaphoreType.DMA((inner,)),
        ],
        (where, *messages, raw, raw2, slope, slope2, turned, point_back, near_ids),
        1,
        far=(slabs + 3,),
        away=(slabs + 3,),
    )
    colour = found[:, :count]
    if split == 2:
        other = lax.ppermute(grad, "view", pairing)
        colour = colour + lax.ppermute(found[:, count:], "view", pairing)
        grad = jnp.where(
            half == 0,
            jnp.concatenate([grad, other], axis=1),
            jnp.concatenate([other, grad], axis=1),
        )
    return (colour[None], grad.reshape(chans, depth, cells))


def solution(mesh):
    in_specs = (P(None, "slab", None), P(), P(), P(), P("view", None), P("view", None, "slab"))
    out_specs = (P("view", None, "slab"), P(None, "slab", None))
    return jax.shard_map(
        on_device, mesh=mesh, in_specs=in_specs, out_specs=out_specs, check_vma=False
    )
```

```python
import functools

import jax
import jax.numpy as jnp
from jax import lax
from jax.experimental import pallas as pl
from jax.experimental.pallas import tpu as pltpu
from jax.sharding import PartitionSpec as P

CX = 32
CY = 32
F32 = jnp.float32
BF16 = jnp.bfloat16
VMEM_LIMIT = 24 * 1024 * 1024
VM = pl.BlockSpec(memory_space=pltpu.VMEM)
SM = pl.BlockSpec(memory_space=pltpu.SMEM)


def rows_of(split):
    if split == 1:
        return CX
    return min(CX, -(-(CX // split + 1) // 4) * 4)


def lane_shift(x, amount, y):
    width = x.shape[-1]
    moved = pltpu.roll(x, (-amount) % width, 1)
    if amount == 1:
        keep = y < CY - 1
    elif amount == -1:
        keep = y > 0
    else:
        lane = lax.broadcasted_iota(jnp.int32, x.shape, 1)
        keep = lane < width - CY if amount > 0 else lane >= CY
    return jnp.where(keep, moved, 0.0)


def thirds(x):
    high = x.astype(BF16)
    rest = x - high.astype(F32)
    mid = rest.astype(BF16)
    low = (rest - mid.astype(F32)).astype(BF16)
    return jnp.concatenate([high, mid, low], axis=0)


def softplus(x):
    return jnp.maximum(x, 0.0) + jnp.log1p(jnp.exp(-jnp.abs(x)))


def partner(slab, k, slabs):
    if slabs & (slabs - 1) == 0:
        return slab ^ k
    return (slab - k + slabs) % slabs


def swap(x):
    return pltpu.roll(x, 4, 0)


def spread(x, put):
    chans, width = x.shape
    lane = lax.broadcasted_iota(jnp.int32, (chans, width), 1)

    def keep(inside):
        return jnp.where(inside, 1.0, 0.0).astype(BF16)

    before = pltpu.roll(x * keep(lane % CY != CY - 1), 1, 1)
    after = pltpu.roll(x * keep(lane % CY != 0), width - 1, 1)
    for j, by_y in enumerate((before, x, after)):
        put(chans * j, pltpu.roll(by_y * keep(lane < width - CY), CY, 1))
        put(chans * (3 + j), by_y)
        put(chans * (6 + j), pltpu.roll(by_y * keep(lane >= CY), width - CY, 1))


def composed(taps, depth, e):
    total = None
    for a in range(2):
        for b in range(2):
            for c in range(2):
                d = (a + 2 - e[0], b + 2 - e[1], c + 2 - e[2])
                if min(d) >= 0 and max(d) <= 2:
                    at = 9 * d[0] + 3 * d[1] + d[2]
                    term = depth[at : at + 1, :] * taps[4 * a + 2 * b + c]
                    total = term if total is None else total + term
    return total


def near(parity):
    return (-1, 0) if parity == 0 else (0, 1)


def decode_pair(layers, wide_ref, point, slope_ref, raw_ref, k):
    chans = wide_ref.shape[1] // 4
    features = []
    for b in range(2):
        for c in range(2):
            around = jnp.concatenate(
                [
                    layers[j](chans * (3 * (nx + 1) + ny + 1))
                    for j in range(2)
                    for nx in near(b)
                    for ny in near(c)
                ],
                axis=0,
            )
            dw = jnp.dot(wide_ref[2 * b + c], around, preferred_element_type=F32)
            dw = dw[: 2 * chans] + dw[2 * chans :]
            sig = jax.nn.sigmoid(dw)
            silu = dw * sig
            row = 2 * chans * (2 * b + c)
            slope_ref[k, row : row + 2 * chans, :] = silu + sig * (1.0 - silu)
            features.append(silu.astype(BF16))
    raw_ref[k] = jnp.dot(point, jnp.concatenate(features, axis=0), preferred_element_type=F32)


def taps_and_depth(tconv_ref, depth_ref, taps_ref, depth_pad_ref):
    chans = tconv_ref.shape[0]
    taps_ref[:, 0:chans] = tconv_ref[...].astype(F32).reshape(8 * chans, chans)
    taps = [taps_ref[pl.ds(q, chans, stride=8), :][:, :chans] for q in range(8)]
    depth_pad_ref[:, 0:27] = depth_ref[...]
    return taps, depth_pad_ref[...].T


def point_lines(weight_ref):
    chans = weight_ref.shape[1]
    weight = weight_ref[...].astype(F32)
    lines = jnp.concatenate([weight] * 8, axis=1)
    lines = jnp.concatenate([jnp.broadcast_to(lines[o : o + 1], (8, 8 * chans)) for o in range(4)], axis=0)
    row = lax.broadcasted_iota(jnp.int32, lines.shape, 0) % 8
    col = lax.broadcasted_iota(jnp.int32, lines.shape, 1) // chans
    return jnp.where(col == 2 * (row % 4) + row // 4, lines, 0.0)


def weight_kernel(tconv_ref, depth_ref, weight_ref, wide_ref, point_ref, taps_ref, depth_pad_ref, full_ref):
    chans = tconv_ref.shape[0]
    taps, depth = taps_and_depth(tconv_ref, depth_ref, taps_ref, depth_pad_ref)
    for b in range(2):
        for c in range(2):
            for first in range(2):
                for j in range(2):
                    for nx in near(b):
                        for ny in near(c):
                            e = (2 - 2 * j + first, b - 2 * nx + 1, c - 2 * ny + 1)
                            at = chans * (4 * j + 2 * (nx - near(b)[0]) + ny - near(c)[0])
                            col = chans * first
                            full_ref[2 * b + c, at : at + chans, col : col + chans] = composed(taps, depth, e)
            whole = full_ref[2 * b + c].T[: 2 * chans]
            high = whole.astype(BF16)
            wide_ref[2 * b + c, : 2 * chans, :] = high
            wide_ref[2 * b + c, 2 * chans :, :] = (whole - high.astype(F32)).astype(BF16)
    point_ref[...] = point_lines(weight_ref).astype(BF16)


def turn_kernel(tconv_ref, depth_ref, weight_ref, _, turned_ref, back_ref, taps_ref, depth_pad_ref, full2_ref):
    chans = tconv_ref.shape[0]
    taps, depth = taps_and_depth(tconv_ref, depth_ref, taps_ref, depth_pad_ref)
    full2_ref[...] = jnp.zeros_like(full2_ref)
    for b in range(2):
        for n in range(2):
            nx = n - b
            for ny in (-1, 0, 1):
                row = chans * (3 * n + ny + 1)
                for j in range(4):
                    for c in range(2):
                        e = (j, 2 * nx + b + 1, 2 * ny + c + 1)
                        if 0 <= e[2] < 4:
                            col = chans * (4 * (j // 2) + 2 * c + j % 2)
                            full2_ref[b, row : row + chans, col : col + chans] = composed(taps, depth, e)
    turned_ref[...] = full2_ref[...].astype(BF16)
    turned = point_lines(weight_ref).T
    back_ref[...] = jnp.concatenate([turned] * 3, axis=1).astype(BF16)


def pack_kernel(where_ref, window_ref, targets_ref, ids_ref, one_ref, two_ref):
    depth, chans, width = window_ref.shape
    count = targets_ref.shape[2]
    slab = where_ref[0]
    even = lax.rem(slab, 2) == 0
    first, last = window_ref[0].astype(F32), window_ref[depth - 1].astype(F32)
    ids = ids_ref[:, pl.ds(pl.multiple_of(slab * count, 128), count)].astype(F32)
    block = jnp.concatenate([targets_ref[0], targets_ref[1], targets_ref[2], ids], axis=0)
    rows = jnp.concatenate([thirds(block).astype(F32), jnp.zeros((4, count), F32)], axis=0)
    rows = jnp.concatenate([rows, jnp.zeros((16, width - count), F32)], axis=1).astype(BF16)
    one_ref[0:chans, :] = jnp.where(even, last, first).astype(BF16)
    two_ref[0:chans, :] = jnp.where(even, first, last).astype(BF16)
    one_ref[chans : chans + 16, :] = rows
    two_ref[chans : chans + 16, :] = rows


def block_at(ref, j, count):
    x = ref[:, count * j : count * (j + 1)].astype(F32)
    return x[0:4] + x[4:8] + x[8:12]


def inner_kernel(lat_ref, wide_ref, point_ref, away_ref, raw_ref, edge_ref, x9_ref, slope_ref, sems):
    layers, chans, width = lat_ref.shape


    def layer(k):
        def put(at, block):
            x9_ref[k, at : at + chans, :] = block

        spread(lat_ref[k], put)

    layer(0)
    for k in range(layers - 1):
        layer(k + 1)
        around = [lambda at, j=j: x9_ref[k + j, at : at + chans, :] for j in range(2)]
        decode_pair(around, wide_ref, point_ref[...], slope_ref, raw_ref, k)
        pltpu.make_async_copy(slope_ref.at[k], away_ref.at[k], sems.at[k]).start()
    edge_ref[0] = x9_ref[0]
    edge_ref[1] = x9_ref[layers - 1]
    for k in range(layers - 1):
        pltpu.make_async_copy(slope_ref.at[k], away_ref.at[k], sems.at[k]).wait()


def outer_kernel(
    scale, where_ref, one_ref, two_ref, edge_ref, wide_ref, point_ref, inner_ref,
    slope_ref, raw_ref, tot_ref, x9_ref,
):
    slab, slabs = where_ref[0], where_ref[3]
    width = one_ref.shape[1]
    chans = edge_ref.shape[1] // 9
    pairs = inner_ref.shape[0] + 2
    even = lax.rem(slab, 2) == 0
    one, two = one_ref[0:chans, :].astype(F32), two_ref[0:chans, :].astype(F32)
    low = jnp.where(slab == 0, 0.0, jnp.where(even, two, one))
    high = jnp.where(slab == slabs - 1, 0.0, jnp.where(even, one, two))
    for k, x in ((0, low), (1, high)):

        def put(at, block, k=k):
            x9_ref[k, at : at + chans, :] = block

        spread(x.astype(BF16), put)
        layers = [lambda at, k=k: x9_ref[k, at : at + chans, :], lambda at, k=k: edge_ref[k, at : at + chans, :]]
        decode_pair(layers if k == 0 else layers[::-1], wide_ref, point_ref[...], slope_ref, raw_ref, k)
    second = lax.broadcasted_iota(jnp.int32, (8, width), 0) >= 4
    before = jnp.zeros((8, width), F32)
    colour = [jnp.zeros((8, width), F32) for _ in range(3)]
    for k in range(pairs):
        raw = raw_at(raw_ref, inner_ref, k)
        tau = softplus(raw[0:8]) * scale
        if k == 0:
            tau = jnp.where(second, tau, 0.0)
        if k == pairs - 1:
            tau = jnp.where(second, 0.0, tau)
        other = swap(tau)
        weight = jnp.exp(-(before + jnp.where(second, other, 0.0))) * (1.0 - jnp.exp(-tau))
        before = before + (tau + other)
        for o in range(3):
            colour[o] = colour[o] + weight * jax.nn.sigmoid(raw[8 * o + 8 : 8 * o + 16])
    colour = [c + swap(c) for c in colour]
    tot_ref[0:8, :] = jnp.where(second, colour[0], before)
    tot_ref[8:16, :] = jnp.where(second, colour[2], colour[1])


def raw_at(outer_ref, inner_ref, k):
    last = inner_ref.shape[0] + 1
    if k == 0:
        return outer_ref[0]
    if k == last:
        return outer_ref[1]
    return inner_ref[k - 1]


def cell_of(ids):
    fine_x, fine_y = ids // (2 * CY), ids % (2 * CY)
    return (fine_x // 2) * CY + fine_y // 2, (fine_x % 2) * 2 + fine_y % 2


def target_kernel(count, where_ref, tot_ref, *refs):
    *block_refs, msg_ref, near_ref = refs
    width = tot_ref.shape[1]
    start = where_ref[1]
    msg_ref[0:16, :] = tot_ref[...]
    row = lax.broadcasted_iota(jnp.int32, (16, count), 0)
    cells = lax.broadcasted_iota(jnp.int32, (count, width), 1)
    total = jnp.zeros((48, width), F32)
    for i, ref in enumerate(block_refs):
        for j in range(ref.shape[1] // count):
            block = block_at(ref, j, count)
            if j == 0:
                near_ref[:, count * i : count * (i + 1)] = block[3:4, :].astype(jnp.int32)
            cell, part = cell_of(block[3:4, :].astype(jnp.int32))
            value = jnp.where(row < 4, 1.0, jnp.where(row < 8, block[0:1, :], jnp.where(row < 12, block[1:2, :], block[2:3, :])))
            value = jnp.where(row % 4 == part, value, 0.0)
            column = jnp.broadcast_to(cell - start, (8, count)).astype(F32).T[:, 0:1].astype(jnp.int32)
            hot = jnp.where(cells == column, 1.0, 0.0).astype(BF16)
            total = total + jnp.dot(thirds(value), hot, preferred_element_type=F32)
    msg_ref[16:32, :] = total[0:16] + (total[16:32] + total[32:48])


def back_kernel(scale, where_ref, *refs):
    (*msg_refs, inner_ref, outer_ref, away_ref, slope2_ref, wide_ref, point_ref, near_ref) = refs[:-8]
    grad_ref, colour_ref, gdw_ref, e_ref, w_ref, tile_ref, slope_ref, sems = refs[-8:]
    slab, start, own_start = where_ref[0], where_ref[1], where_ref[2]
    slabs = len(msg_refs)
    inner, _, width = inner_ref.shape
    pairs = inner + 2
    chans = slope_ref.shape[1] // 8
    own_width = grad_ref.shape[1]
    second = lax.broadcasted_iota(jnp.int32, (8, width), 0) >= 4
    cuts = (0, inner // 3, 2 * inner // 3, inner)
    loads = [
        pltpu.make_async_copy(away_ref.at[a:b], slope_ref.at[a:b], sems.at[i])
        for i, (a, b) in enumerate(zip(cuts, cuts[1:]))
    ]
    for load in loads:
        load.start()

    def both(x):
        other = swap(x)
        return jnp.where(second, other, x), jnp.where(second, x, other)

    totals, colours, hits = [], [], None
    for ref in msg_refs:
        tau_total, c0 = both(ref[0:8, :])
        c1, c2 = both(ref[8:16, :])
        totals.append(tau_total)
        colours.append((c0, c1, c2))
        here = (ref[16:24, :], ref[24:32, :])
        hits = here if hits is None else (hits[0] + here[0], hits[1] + here[1])
    index = [partner(slab, k, slabs) for k in range(slabs)]
    full = [jnp.zeros((8, width), F32) for _ in range(3)]
    after = [jnp.zeros((8, width), F32) for _ in range(3)]
    prefix = None
    for k in range(slabs):
        ahead = jnp.zeros((8, width), F32)
        for other in range(slabs):
            if other != k:
                ahead = ahead + jnp.where(index[other] < index[k], totals[other], 0.0)
        if k == 0:
            prefix = ahead
        through = jnp.exp(-ahead)
        for o in range(3):
            part = through * colours[k][o]
            full[o] = full[o] + part
            if k:
                after[o] = after[o] + jnp.where(index[k] > slab, part, 0.0)
    number, t0 = both(hits[0])
    t1, t2 = both(hits[1])
    pull = [number * full[o] - t for o, t in enumerate((t0, t1, t2))]

    tau0 = softplus(outer_ref[0, 0:8, :]) * scale
    before = -both(tau0)[0]
    for k in range(pairs):
        tau = softplus(raw_at(outer_ref, inner_ref, k)[0:8]) * scale
        other = swap(tau)
        through = jnp.exp(-(prefix + (before + jnp.where(second, other, 0.0))))
        before = before + (tau + other)
        left = jnp.exp(-tau)
        w_ref[k, 0:8, :] = through * (1.0 - left)
        w_ref[k, 8:16, :] = through * left
    last = pairs - 1
    for o in range(3):
        e = w_ref[last, 0:8, :] * jax.nn.sigmoid(outer_ref[1, 8 * o + 8 : 8 * o + 16, :])
        after[o] = after[o] - both(e)[1]
    for k in range(pairs - 1, -1, -1):
        weight, later = w_ref[k, 0:8, :], w_ref[k, 8:16, :]
        raw = raw_at(outer_ref, inner_ref, k)
        total = jnp.zeros((8, width), F32)
        outside = None
        if k == 0:
            outside = jnp.logical_and(jnp.logical_not(second), slab == 0)
        if k == last:
            outside = jnp.logical_and(second, slab == slabs - 1)
        for o in range(3):
            rgb = jax.nn.sigmoid(raw[8 * o + 8 : 8 * o + 16])
            e = weight * rgb
            other = swap(e)
            rest = after[o] + jnp.where(second, 0.0, other)
            after[o] = after[o] + (e + other)
            total = total + pull[o] * (later * rgb - rest)
            grad = pull[o] * (e * (1.0 - rgb))
            if outside is not None:
                grad = jnp.where(outside, 0.0, grad)
            e_ref[k, 8 * o + 8 : 8 * o + 16, :] = grad
        grad = total * (scale * jax.nn.sigmoid(raw[0:8]))
        if outside is not None:
            grad = jnp.where(outside, 0.0, grad)
        e_ref[k, 0:8, :] = grad

    count = near_ref.shape[1]
    cell, part = cell_of(near_ref[...])
    cell = cell - own_start
    mine = jnp.logical_and(cell >= 0, cell < own_width)
    cell = jnp.where(mine, cell + (own_start - start), -1)
    hot = jnp.where(lax.broadcasted_iota(jnp.int32, (width, count), 0) == cell, 1.0, 0.0).astype(BF16)
    rows = jnp.concatenate(
        [jnp.where(second, full[1], full[0]), jnp.where(second, full[2], full[2])], axis=0
    )
    found = jnp.dot(thirds(rows), hot, preferred_element_type=F32)
    found = found[0:16] + (found[16:32] + found[32:48])
    row = lax.broadcasted_iota(jnp.int32, (16, count), 0)
    found = jnp.where(row % 4 == part, found, 0.0)
    for o in range(3):
        colour_ref[o : o + 1, :] = jnp.sum(found[4 * o : 4 * o + 4], axis=0, keepdims=True)

    def pair(k):
        if k - 1 in cuts[:-1]:
            loads[cuts.index(k - 1)].wait()
        slope = slope_ref[k - 1] if 0 < k < last else slope2_ref[k // last]
        grad_features = jnp.dot(point_ref[...], thirds(e_ref[k]), preferred_element_type=F32)
        gdw_ref[k] = (grad_features * slope).astype(BF16)

    y = lax.broadcasted_iota(jnp.int32, (chans, width), 1) % CY
    low = own_start == start
    for k in (0, last, *range(1, last)):
        pair(k)
    for z in range(pairs - 1):
        every = []
        for b in range(2):
            at = 4 * chans * b
            around = gdw_ref[z : z + 2, at : at + 4 * chans, :].reshape(8 * chans, width)
            every.append(jnp.dot(wide_ref[b], around, preferred_element_type=F32))
        total = None
        for j in range(3):
            at = chans * j
            line = every[0][at : at + chans] + every[1][at + 3 * chans : at + 4 * chans]
            line = line + lane_shift(every[1][at : at + chans], -CY, y)
            line = line + lane_shift(every[0][at + 3 * chans : at + 4 * chans], CY, y)
            if j != 1:
                line = lane_shift(line, j - 1, y)
            total = line if total is None else total + line
        if own_width < width:
            total = jnp.where(low, total[:, :own_width], total[:, width - own_width :])
        for t in range(own_width // 128):
            tile_ref[t, pl.ds(z, chans, stride=pairs - 1), :] = total[:, 128 * t : 128 * t + 128]
    for t in range(own_width // 128):
        grad_ref[:, 128 * t : 128 * t + 128] = tile_ref[t]


def call(kernel, outs, scratch, operands, smem, far=(), away=(), away_out=None):
    operands = list(operands)
    specs = [SM] * smem + [VM] * (len(operands) - smem)
    out_specs = [VM] * len(outs)
    shapes = [jax.ShapeDtypeStruct(s, t) for s, t in outs]
    for i in far:
        operands[i] = pltpu.with_memory_space_constraint(operands[i], pltpu.HBM)
    for i in away:
        specs[i] = pl.BlockSpec(memory_space=pltpu.HBM)
    if away_out is not None:
        shapes[away_out] = pltpu.HBM(*outs[away_out])
        out_specs[away_out] = pl.BlockSpec(memory_space=pltpu.HBM)
    return pl.pallas_call(
        kernel,
        out_shape=shapes,
        in_specs=specs,
        out_specs=out_specs,
        scratch_shapes=[pltpu.VMEM(*x) if isinstance(x, tuple) else x for x in scratch],
        compiler_params=pltpu.CompilerParams(vmem_limit_bytes=VMEM_LIMIT),
    )(*operands)


def on_device(latent, tconv_weight, depth_weight, point_weight, pencil_ids, targets):
    chans, depth, cells = latent.shape
    view, slab = lax.axis_index("view"), lax.axis_index("slab")
    views, slabs = lax.axis_size("view"), lax.axis_size("slab")
    count = targets.shape[2]
    split = 2 if views % 2 == 0 else 1
    rows = rows_of(split)
    width, own_width = rows * CY, cells // split
    half = view % split
    start = half * (cells - width)
    own_start = half * own_width
    where = jnp.stack([slab, start, own_start, slabs]).astype(jnp.int32)
    scale = 1.5 / (2 * depth * slabs)

    window = lax.dynamic_slice_in_dim(jnp.transpose(latent, (1, 0, 2)), start, width, axis=2)
    one, two = call(
        pack_kernel,
        [((chans + 16, width), BF16)] * 2,
        [],
        (where, window, jnp.transpose(targets, (1, 0, 2)), pencil_ids),
        1,
        far=(2, 3),
    )

    def send(x, mask, partner):
        pairs = [(v * slabs + s, (v ^ mask) * slabs + partner(s)) for v in range(views) for s in range(slabs)]
        return lax.ppermute(x, ("view", "slab"), pairs)

    small = (jnp.transpose(tconv_weight, (0, 2, 1)), depth_weight, point_weight)
    room = [((8 * chans, 128), F32), ((chans, 128), F32)]
    wide, point = call(
        weight_kernel,
        [((4, 4 * chans, 8 * chans), BF16), ((32, 8 * chans), BF16)],
        [*room, ((4, 8 * chans, 128), F32)],
        small,
        0,
        far=(0, 1, 2),
    )

    chips = views // split
    blocks = [one[chans:, :count]]
    one = send(one, split if chips > 1 else 0, lambda s: (s + 1 - 2 * (s % 2)) % slabs)
    two = send(two, 2 * split if chips > 2 else 0, lambda s: (s + 2 * (s % 2) - 1) % slabs)
    rest = [send(blocks[0], m * split, lambda s: s) for m in range(3, chips)]
    inner = depth - 1
    slope, raw, edge = call(
        inner_kernel,
        [((inner, 8 * chans, width), F32), ((inner, 32, width), F32), ((2, 9 * chans, width), BF16)],
        [
            ((depth, 9 * chans, width), BF16),
            ((inner, 8 * chans, width), F32),
            pltpu.SemaphoreType.DMA((inner,)),
        ],
        (window, wide, point),
        0,
        away_out=0,
    )
    one, two, rest, raw, edge = lax.optimization_barrier((one, two, rest, raw, edge))
    blocks += [one[chans:, :count], two[chans:, :count]][: chips - 1]
    blocks = jnp.concatenate(blocks + rest, axis=1)
    groups = [blocks]
    if split == 2:
        pairing = [(i, i ^ 1) for i in range(views)]
        groups.append(lax.ppermute(blocks, "view", pairing))
    slope2, raw2, tot = call(
        functools.partial(outer_kernel, scale),
        [((2, 8 * chans, width), F32), ((2, 32, width), F32), ((16, width), F32)],
        [((2, 9 * chans, width), BF16)],
        (where, one, two, edge, wide, point, raw),
        1,
    )
    message, near_ids = call(
        functools.partial(target_kernel, count),
        [((32, width), F32), ((1, split * count), jnp.int32)],
        [],
        (where, tot, *groups),
        1,
    )
    messages = [message]
    for k in range(1, slabs):
        messages.append(lax.ppermute(message, "slab", [(partner(i, k, slabs), i) for i in range(slabs)]))
    turned, point_back = call(
        turn_kernel,
        [((2, 6 * chans, 8 * chans), BF16), ((8 * chans, 96), BF16)],
        [*room, ((2, 6 * chans, 8 * chans), F32)],
        (*small, message),
        0,
        far=(0, 1, 2),
    )
    grad, found = call(
        functools.partial(back_kernel, scale),
        [((chans * depth, own_width), F32), ((3, split * count), F32)],
        [
            ((inner + 2, 8 * chans, width), BF16),
            ((inner + 2, 32, width), F32),
            ((inner + 2, 16, width), F32),
            ((own_width // 128, chans * depth, 128), F32),
            ((inner, 8 * chans, width), F32),
            pltpu.SemaphoreType.DMA((inner,)),
        ],
        (where, *messages, raw, raw2, slope, slope2, turned, point_back, near_ids),
        1,
        far=(slabs + 3,),
        away=(slabs + 3,),
    )
    colour = found[:, :count]
    if split == 2:
        other = lax.ppermute(grad, "view", pairing)
        colour = colour + lax.ppermute(found[:, count:], "view", pairing)
        grad = jnp.where(
            half == 0,
            jnp.concatenate([grad, other], axis=1),
            jnp.concatenate([other, grad], axis=1),
        )
    return (colour[None], grad.reshape(chans, depth, cells))


def solution(mesh):
    in_specs = (P(None, "slab", None), P(), P(), P(), P("view", None), P("view", None, "slab"))
    out_specs = (P("view", None, "slab"), P(None, "slab", None))
    return jax.shard_map(
        on_device, mesh=mesh, in_specs=in_specs, out_specs=out_specs, check_vma=False
    )
```

```python
import functools

import jax
import jax.numpy as jnp
from jax import lax
from jax.experimental import pallas as pl
from jax.experimental.pallas import tpu as pltpu
from jax.sharding import PartitionSpec as P

CX = 32
CY = 32
F32 = jnp.float32
BF16 = jnp.bfloat16
VMEM_LIMIT = 24 * 1024 * 1024
VM = pl.BlockSpec(memory_space=pltpu.VMEM)
SM = pl.BlockSpec(memory_space=pltpu.SMEM)


def rows_of(split):
    if split == 1:
        return CX
    return min(CX, -(-(CX // split + 1) // 4) * 4)


def lane_shift(x, amount, y):
    width = x.shape[-1]
    moved = pltpu.roll(x, (-amount) % width, 1)
    if amount == 1:
        keep = y < CY - 1
    elif amount == -1:
        keep = y > 0
    else:
        lane = lax.broadcasted_iota(jnp.int32, x.shape, 1)
        keep = lane < width - CY if amount > 0 else lane >= CY
    return jnp.where(keep, moved, 0.0)


def thirds(x):
    high = x.astype(BF16)
    rest = x - high.astype(F32)
    mid = rest.astype(BF16)
    low = (rest - mid.astype(F32)).astype(BF16)
    return jnp.concatenate([high, mid, low], axis=0)


def softplus(x):
    return jnp.maximum(x, 0.0) + jnp.log1p(jnp.exp(-jnp.abs(x)))


def partner(slab, k, slabs):
    if slabs & (slabs - 1) == 0:
        return slab ^ k
    return (slab - k + slabs) % slabs


def swap(x):
    return pltpu.roll(x, 4, 0)


def spread(x, put):
    chans, width = x.shape
    lane = lax.broadcasted_iota(jnp.int32, (chans, width), 1)

    def keep(inside):
        return jnp.where(inside, 1.0, 0.0).astype(BF16)

    before = pltpu.roll(x * keep(lane % CY != CY - 1), 1, 1)
    after = pltpu.roll(x * keep(lane % CY != 0), width - 1, 1)
    for j, by_y in enumerate((before, x, after)):
        put(chans * j, pltpu.roll(by_y * keep(lane < width - CY), CY, 1))
        put(chans * (3 + j), by_y)
        put(chans * (6 + j), pltpu.roll(by_y * keep(lane >= CY), width - CY, 1))


def composed(taps, depth, e):
    total = None
    for a in range(2):
        for b in range(2):
            for c in range(2):
                d = (a + 2 - e[0], b + 2 - e[1], c + 2 - e[2])
                if min(d) >= 0 and max(d) <= 2:
                    at = 9 * d[0] + 3 * d[1] + d[2]
                    term = depth[at : at + 1, :] * taps[4 * a + 2 * b + c]
                    total = term if total is None else total + term
    return total


def near(parity):
    return (-1, 0) if parity == 0 else (0, 1)


def decode_pair(layers, wide_ref, point, slope_ref, raw_ref, k):
    chans = wide_ref.shape[1] // 4
    features = []
    for b in range(2):
        for c in range(2):
            around = jnp.concatenate(
                [
                    layers[j](chans * (3 * (nx + 1) + ny + 1))
                    for j in range(2)
                    for nx in near(b)
                    for ny in near(c)
                ],
                axis=0,
            )
            dw = jnp.dot(wide_ref[2 * b + c], around, preferred_element_type=F32)
            dw = dw[: 2 * chans] + dw[2 * chans :]
            sig = jax.nn.sigmoid(dw)
            silu = dw * sig
            row = 2 * chans * (2 * b + c)
            slope_ref[k, row : row + 2 * chans, :] = silu + sig * (1.0 - silu)
            features.append(silu.astype(BF16))
    raw_ref[k] = jnp.dot(point, jnp.concatenate(features, axis=0), preferred_element_type=F32)


def taps_and_depth(tconv_ref, depth_ref, taps_ref, depth_pad_ref):
    chans = tconv_ref.shape[0]
    taps_ref[:, 0:chans] = tconv_ref[...].astype(F32).reshape(8 * chans, chans)
    taps = [taps_ref[pl.ds(q, chans, stride=8), :][:, :chans] for q in range(8)]
    depth_pad_ref[:, 0:27] = depth_ref[...]
    return taps, depth_pad_ref[...].T


def point_lines(weight_ref):
    chans = weight_ref.shape[1]
    weight = weight_ref[...].astype(F32)
    lines = jnp.concatenate([weight] * 8, axis=1)
    lines = jnp.concatenate([jnp.broadcast_to(lines[o : o + 1], (8, 8 * chans)) for o in range(4)], axis=0)
    row = lax.broadcasted_iota(jnp.int32, lines.shape, 0) % 8
    col = lax.broadcasted_iota(jnp.int32, lines.shape, 1) // chans
    return jnp.where(col == 2 * (row % 4) + row // 4, lines, 0.0)


def weight_kernel(tconv_ref, depth_ref, weight_ref, wide_ref, point_ref, taps_ref, depth_pad_ref, full_ref):
    chans = tconv_ref.shape[0]
    taps, depth = taps_and_depth(tconv_ref, depth_ref, taps_ref, depth_pad_ref)
    for b in range(2):
        for c in range(2):
            for first in range(2):
                for j in range(2):
                    for nx in near(b):
                        for ny in near(c):
                            e = (2 - 2 * j + first, b - 2 * nx + 1, c - 2 * ny + 1)
                            at = chans * (4 * j + 2 * (nx - near(b)[0]) + ny - near(c)[0])
                            col = chans * first
                            full_ref[2 * b + c, at : at + chans, col : col + chans] = composed(taps, depth, e)
            whole = full_ref[2 * b + c].T[: 2 * chans]
            high = whole.astype(BF16)
            wide_ref[2 * b + c, : 2 * chans, :] = high
            wide_ref[2 * b + c, 2 * chans :, :] = (whole - high.astype(F32)).astype(BF16)
    point_ref[...] = point_lines(weight_ref).astype(BF16)


def turn_kernel(tconv_ref, depth_ref, weight_ref, _, turned_ref, back_ref, taps_ref, depth_pad_ref, full2_ref):
    chans = tconv_ref.shape[0]
    taps, depth = taps_and_depth(tconv_ref, depth_ref, taps_ref, depth_pad_ref)
    full2_ref[...] = jnp.zeros_like(full2_ref)
    for b in range(2):
        for n in range(2):
            nx = n - b
            for ny in (-1, 0, 1):
                row = chans * (3 * n + ny + 1)
                for j in range(4):
                    for c in range(2):
                        e = (j, 2 * nx + b + 1, 2 * ny + c + 1)
                        if 0 <= e[2] < 4:
                            col = chans * (4 * (j // 2) + 2 * c + j % 2)
                            full2_ref[b, row : row + chans, col : col + chans] = composed(taps, depth, e)
    turned_ref[...] = full2_ref[...].astype(BF16)
    turned = point_lines(weight_ref).T
    back_ref[...] = jnp.concatenate([turned] * 3, axis=1).astype(BF16)


def pack_kernel(where_ref, window_ref, targets_ref, ids_ref, one_ref, two_ref):
    depth, chans, width = window_ref.shape
    count = targets_ref.shape[2]
    slab = where_ref[0]
    even = lax.rem(slab, 2) == 0
    first, last = window_ref[0].astype(F32), window_ref[depth - 1].astype(F32)
    ids = ids_ref[:, pl.ds(pl.multiple_of(slab * count, 128), count)].astype(F32)
    block = jnp.concatenate([targets_ref[0], targets_ref[1], targets_ref[2], ids], axis=0)
    rows = jnp.concatenate([thirds(block).astype(F32), jnp.zeros((4, count), F32)], axis=0)
    rows = jnp.concatenate([rows, jnp.zeros((16, width - count), F32)], axis=1).astype(BF16)
    one_ref[0:chans, :] = jnp.where(even, last, first).astype(BF16)
    two_ref[0:chans, :] = jnp.where(even, first, last).astype(BF16)
    one_ref[chans : chans + 16, :] = rows
    two_ref[chans : chans + 16, :] = rows


def block_at(ref, j, count):
    x = ref[:, count * j : count * (j + 1)].astype(F32)
    return x[0:4] + x[4:8] + x[8:12]


def inner_kernel(lat_ref, wide_ref, point_ref, away_ref, raw_ref, edge_ref, near_ref, x9_ref, slope_ref, sems):
    layers, chans, width = lat_ref.shape


    def layer(k):
        def put(at, block):
            x9_ref[k, at : at + chans, :] = block

        spread(lat_ref[k], put)

    layer(0)
    for k in range(layers - 1):
        layer(k + 1)
        around = [lambda at, j=j: x9_ref[k + j, at : at + chans, :] for j in range(2)]
        decode_pair(around, wide_ref, point_ref[...], slope_ref, raw_ref, k)
        if k < layers - 2:
            pltpu.make_async_copy(slope_ref.at[k], away_ref.at[k], sems.at[k]).start()
    edge_ref[0] = x9_ref[0]
    edge_ref[1] = x9_ref[layers - 1]
    near_ref[...] = slope_ref[layers - 2]
    for k in range(layers - 2):
        pltpu.make_async_copy(slope_ref.at[k], away_ref.at[k], sems.at[k]).wait()


def outer_kernel(
    scale, where_ref, one_ref, two_ref, edge_ref, wide_ref, point_ref, inner_ref,
    slope_ref, raw_ref, tot_ref, x9_ref,
):
    slab, slabs = where_ref[0], where_ref[3]
    width = one_ref.shape[1]
    chans = edge_ref.shape[1] // 9
    pairs = inner_ref.shape[0] + 2
    even = lax.rem(slab, 2) == 0
    one, two = one_ref[0:chans, :].astype(F32), two_ref[0:chans, :].astype(F32)
    low = jnp.where(slab == 0, 0.0, jnp.where(even, two, one))
    high = jnp.where(slab == slabs - 1, 0.0, jnp.where(even, one, two))
    for k, x in ((0, low), (1, high)):

        def put(at, block, k=k):
            x9_ref[k, at : at + chans, :] = block

        spread(x.astype(BF16), put)
        layers = [lambda at, k=k: x9_ref[k, at : at + chans, :], lambda at, k=k: edge_ref[k, at : at + chans, :]]
        decode_pair(layers if k == 0 else layers[::-1], wide_ref, point_ref[...], slope_ref, raw_ref, k)
    second = lax.broadcasted_iota(jnp.int32, (8, width), 0) >= 4
    before = jnp.zeros((8, width), F32)
    colour = [jnp.zeros((8, width), F32) for _ in range(3)]
    for k in range(pairs):
        raw = raw_at(raw_ref, inner_ref, k)
        tau = softplus(raw[0:8]) * scale
        if k == 0:
            tau = jnp.where(second, tau, 0.0)
        if k == pairs - 1:
            tau = jnp.where(second, 0.0, tau)
        other = swap(tau)
        weight = jnp.exp(-(before + jnp.where(second, other, 0.0))) * (1.0 - jnp.exp(-tau))
        before = before + (tau + other)
        for o in range(3):
            colour[o] = colour[o] + weight * jax.nn.sigmoid(raw[8 * o + 8 : 8 * o + 16])
    colour = [c + swap(c) for c in colour]
    tot_ref[0:8, :] = jnp.where(second, colour[0], before)
    tot_ref[8:16, :] = jnp.where(second, colour[2], colour[1])


def raw_at(outer_ref, inner_ref, k):
    last = inner_ref.shape[0] + 1
    if k == 0:
        return outer_ref[0]
    if k == last:
        return outer_ref[1]
    return inner_ref[k - 1]


def cell_of(ids):
    fine_x, fine_y = ids // (2 * CY), ids % (2 * CY)
    return (fine_x // 2) * CY + fine_y // 2, (fine_x % 2) * 2 + fine_y % 2


def target_kernel(count, where_ref, tot_ref, *refs):
    *block_refs, msg_ref, near_ref = refs
    width = tot_ref.shape[1]
    start = where_ref[1]
    msg_ref[0:16, :] = tot_ref[...]
    row = lax.broadcasted_iota(jnp.int32, (16, count), 0)
    cells = lax.broadcasted_iota(jnp.int32, (count, width), 1)
    total = jnp.zeros((48, width), F32)
    for i, ref in enumerate(block_refs):
        for j in range(ref.shape[1] // count):
            block = block_at(ref, j, count)
            if j == 0:
                near_ref[:, count * i : count * (i + 1)] = block[3:4, :].astype(jnp.int32)
            cell, part = cell_of(block[3:4, :].astype(jnp.int32))
            value = jnp.where(row < 4, 1.0, jnp.where(row < 8, block[0:1, :], jnp.where(row < 12, block[1:2, :], block[2:3, :])))
            value = jnp.where(row % 4 == part, value, 0.0)
            column = jnp.broadcast_to(cell - start, (8, count)).astype(F32).T[:, 0:1].astype(jnp.int32)
            hot = jnp.where(cells == column, 1.0, 0.0).astype(BF16)
            total = total + jnp.dot(thirds(value), hot, preferred_element_type=F32)
    msg_ref[16:32, :] = total[0:16] + (total[16:32] + total[32:48])


def back_kernel(scale, where_ref, *refs):
    (*msg_refs, inner_ref, outer_ref, away_ref, slope2_ref, wide_ref, point_ref, near_ref, slope3_ref) = refs[:-8]
    grad_ref, colour_ref, gdw_ref, e_ref, w_ref, tile_ref, slope_ref, sems = refs[-8:]
    slab, start, own_start = where_ref[0], where_ref[1], where_ref[2]
    slabs = len(msg_refs)
    inner, _, width = inner_ref.shape
    pairs = inner + 2
    chans = slope_ref.shape[1] // 8
    own_width = grad_ref.shape[1]
    second = lax.broadcasted_iota(jnp.int32, (8, width), 0) >= 4
    cuts = (0, (inner - 1) // 3, 2 * (inner - 1) // 3, inner - 1)
    loads = [
        pltpu.make_async_copy(away_ref.at[a:b], slope_ref.at[a:b], sems.at[i])
        for i, (a, b) in enumerate(zip(cuts, cuts[1:]))
    ]
    for load in loads:
        load.start()

    def both(x):
        other = swap(x)
        return jnp.where(second, other, x), jnp.where(second, x, other)

    totals, colours, hits = [], [], None
    for ref in msg_refs:
        tau_total, c0 = both(ref[0:8, :])
        c1, c2 = both(ref[8:16, :])
        totals.append(tau_total)
        colours.append((c0, c1, c2))
        here = (ref[16:24, :], ref[24:32, :])
        hits = here if hits is None else (hits[0] + here[0], hits[1] + here[1])
    index = [partner(slab, k, slabs) for k in range(slabs)]
    full = [jnp.zeros((8, width), F32) for _ in range(3)]
    after = [jnp.zeros((8, width), F32) for _ in range(3)]
    prefix = None
    for k in range(slabs):
        ahead = jnp.zeros((8, width), F32)
        for other in range(slabs):
            if other != k:
                ahead = ahead + jnp.where(index[other] < index[k], totals[other], 0.0)
        if k == 0:
            prefix = ahead
        through = jnp.exp(-ahead)
        for o in range(3):
            part = through * colours[k][o]
            full[o] = full[o] + part
            if k:
                after[o] = after[o] + jnp.where(index[k] > slab, part, 0.0)
    number, t0 = both(hits[0])
    t1, t2 = both(hits[1])
    pull = [number * full[o] - t for o, t in enumerate((t0, t1, t2))]

    tau0 = softplus(outer_ref[0, 0:8, :]) * scale
    before = -both(tau0)[0]
    for k in range(pairs):
        tau = softplus(raw_at(outer_ref, inner_ref, k)[0:8]) * scale
        other = swap(tau)
        through = jnp.exp(-(prefix + (before + jnp.where(second, other, 0.0))))
        before = before + (tau + other)
        left = jnp.exp(-tau)
        w_ref[k, 0:8, :] = through * (1.0 - left)
        w_ref[k, 8:16, :] = through * left
    last = pairs - 1
    for o in range(3):
        e = w_ref[last, 0:8, :] * jax.nn.sigmoid(outer_ref[1, 8 * o + 8 : 8 * o + 16, :])
        after[o] = after[o] - both(e)[1]
    for k in range(pairs - 1, -1, -1):
        weight, later = w_ref[k, 0:8, :], w_ref[k, 8:16, :]
        raw = raw_at(outer_ref, inner_ref, k)
        total = jnp.zeros((8, width), F32)
        outside = None
        if k == 0:
            outside = jnp.logical_and(jnp.logical_not(second), slab == 0)
        if k == last:
            outside = jnp.logical_and(second, slab == slabs - 1)
        for o in range(3):
            rgb = jax.nn.sigmoid(raw[8 * o + 8 : 8 * o + 16])
            e = weight * rgb
            other = swap(e)
            rest = after[o] + jnp.where(second, 0.0, other)
            after[o] = after[o] + (e + other)
            total = total + pull[o] * (later * rgb - rest)
            grad = pull[o] * (e * (1.0 - rgb))
            if outside is not None:
                grad = jnp.where(outside, 0.0, grad)
            e_ref[k, 8 * o + 8 : 8 * o + 16, :] = grad
        grad = total * (scale * jax.nn.sigmoid(raw[0:8]))
        if outside is not None:
            grad = jnp.where(outside, 0.0, grad)
        e_ref[k, 0:8, :] = grad

    count = near_ref.shape[1]
    cell, part = cell_of(near_ref[...])
    cell = cell - own_start
    mine = jnp.logical_and(cell >= 0, cell < own_width)
    cell = jnp.where(mine, cell + (own_start - start), -1)
    hot = jnp.where(lax.broadcasted_iota(jnp.int32, (width, count), 0) == cell, 1.0, 0.0).astype(BF16)
    rows = jnp.concatenate(
        [jnp.where(second, full[1], full[0]), jnp.where(second, full[2], full[2])], axis=0
    )
    found = jnp.dot(thirds(rows), hot, preferred_element_type=F32)
    found = found[0:16] + (found[16:32] + found[32:48])
    row = lax.broadcasted_iota(jnp.int32, (16, count), 0)
    found = jnp.where(row % 4 == part, found, 0.0)
    for o in range(3):
        colour_ref[o : o + 1, :] = jnp.sum(found[4 * o : 4 * o + 4], axis=0, keepdims=True)

    def pair(k):
        if k - 1 in cuts[:-1]:
            loads[cuts.index(k - 1)].wait()
        slope = slope3_ref[...] if k == inner else slope_ref[k - 1] if 0 < k < last else slope2_ref[k // last]
        grad_features = jnp.dot(point_ref[...], thirds(e_ref[k]), preferred_element_type=F32)
        gdw_ref[k] = (grad_features * slope).astype(BF16)

    y = lax.broadcasted_iota(jnp.int32, (chans, width), 1) % CY
    low = own_start == start
    for k in (0, last, inner, *range(1, inner)):
        pair(k)
    for z in range(pairs - 1):
        every = []
        for b in range(2):
            at = 4 * chans * b
            around = gdw_ref[z : z + 2, at : at + 4 * chans, :].reshape(8 * chans, width)
            every.append(jnp.dot(wide_ref[b], around, preferred_element_type=F32))
        total = None
        for j in range(3):
            at = chans * j
            line = every[0][at : at + chans] + every[1][at + 3 * chans : at + 4 * chans]
            line = line + lane_shift(every[1][at : at + chans], -CY, y)
            line = line + lane_shift(every[0][at + 3 * chans : at + 4 * chans], CY, y)
            if j != 1:
                line = lane_shift(line, j - 1, y)
            total = line if total is None else total + line
        if own_width < width:
            total = jnp.where(low, total[:, :own_width], total[:, width - own_width :])
        for t in range(own_width // 128):
            tile_ref[t, pl.ds(z, chans, stride=pairs - 1), :] = total[:, 128 * t : 128 * t + 128]
    for t in range(own_width // 128):
        grad_ref[:, 128 * t : 128 * t + 128] = tile_ref[t]


def call(kernel, outs, scratch, operands, smem, far=(), away=(), away_out=None):
    operands = list(operands)
    specs = [SM] * smem + [VM] * (len(operands) - smem)
    out_specs = [VM] * len(outs)
    shapes = [jax.ShapeDtypeStruct(s, t) for s, t in outs]
    for i in far:
        operands[i] = pltpu.with_memory_space_constraint(operands[i], pltpu.HBM)
    for i in away:
        specs[i] = pl.BlockSpec(memory_space=pltpu.HBM)
    if away_out is not None:
        shapes[away_out] = pltpu.HBM(*outs[away_out])
        out_specs[away_out] = pl.BlockSpec(memory_space=pltpu.HBM)
    return pl.pallas_call(
        kernel,
        out_shape=shapes,
        in_specs=specs,
        out_specs=out_specs,
        scratch_shapes=[pltpu.VMEM(*x) if isinstance(x, tuple) else x for x in scratch],
        compiler_params=pltpu.CompilerParams(vmem_limit_bytes=VMEM_LIMIT),
    )(*operands)


def on_device(latent, tconv_weight, depth_weight, point_weight, pencil_ids, targets):
    chans, depth, cells = latent.shape
    view, slab = lax.axis_index("view"), lax.axis_index("slab")
    views, slabs = lax.axis_size("view"), lax.axis_size("slab")
    count = targets.shape[2]
    split = 2 if views % 2 == 0 else 1
    rows = rows_of(split)
    width, own_width = rows * CY, cells // split
    half = view % split
    start = half * (cells - width)
    own_start = half * own_width
    where = jnp.stack([slab, start, own_start, slabs]).astype(jnp.int32)
    scale = 1.5 / (2 * depth * slabs)

    window = lax.dynamic_slice_in_dim(jnp.transpose(latent, (1, 0, 2)), start, width, axis=2)
    one, two = call(
        pack_kernel,
        [((chans + 16, width), BF16)] * 2,
        [],
        (where, window, jnp.transpose(targets, (1, 0, 2)), pencil_ids),
        1,
        far=(2, 3),
    )

    def send(x, mask, partner):
        pairs = [(v * slabs + s, (v ^ mask) * slabs + partner(s)) for v in range(views) for s in range(slabs)]
        return lax.ppermute(x, ("view", "slab"), pairs)

    small = (jnp.transpose(tconv_weight, (0, 2, 1)), depth_weight, point_weight)
    room = [((8 * chans, 128), F32), ((chans, 128), F32)]
    wide, point = call(
        weight_kernel,
        [((4, 4 * chans, 8 * chans), BF16), ((32, 8 * chans), BF16)],
        [*room, ((4, 8 * chans, 128), F32)],
        small,
        0,
        far=(0, 1, 2),
    )

    chips = views // split
    blocks = [one[chans:, :count]]
    one = send(one, split if chips > 1 else 0, lambda s: (s + 1 - 2 * (s % 2)) % slabs)
    two = send(two, 2 * split if chips > 2 else 0, lambda s: (s + 2 * (s % 2) - 1) % slabs)
    rest = [send(blocks[0], m * split, lambda s: s) for m in range(3, chips)]
    inner = depth - 1
    slope, raw, edge, slope3 = call(
        inner_kernel,
        [
            ((inner - 1, 8 * chans, width), F32),
            ((inner, 32, width), F32),
            ((2, 9 * chans, width), BF16),
            ((8 * chans, width), F32),
        ],
        [
            ((depth, 9 * chans, width), BF16),
            ((inner, 8 * chans, width), F32),
            pltpu.SemaphoreType.DMA((inner,)),
        ],
        (window, wide, point),
        0,
        away_out=0,
    )
    one, two, rest, raw, edge = lax.optimization_barrier((one, two, rest, raw, edge))
    blocks += [one[chans:, :count], two[chans:, :count]][: chips - 1]
    blocks = jnp.concatenate(blocks + rest, axis=1)
    groups = [blocks]
    if split == 2:
        pairing = [(i, i ^ 1) for i in range(views)]
        groups.append(lax.ppermute(blocks, "view", pairing))
    slope2, raw2, tot = call(
        functools.partial(outer_kernel, scale),
        [((2, 8 * chans, width), F32), ((2, 32, width), F32), ((16, width), F32)],
        [((2, 9 * chans, width), BF16)],
        (where, one, two, edge, wide, point, raw),
        1,
    )
    message, near_ids = call(
        functools.partial(target_kernel, count),
        [((32, width), F32), ((1, split * count), jnp.int32)],
        [],
        (where, tot, *groups),
        1,
    )
    messages = [message]
    for k in range(slabs - 1, 0, -1):
        sent = lax.ppermute(message, "slab", [(partner(i, k, slabs), i) for i in range(slabs)])
        messages.insert(1, sent)
    turned, point_back = call(
        turn_kernel,
        [((2, 6 * chans, 8 * chans), BF16), ((8 * chans, 96), BF16)],
        [*room, ((2, 6 * chans, 8 * chans), F32)],
        (*small, message),
        0,
        far=(0, 1, 2),
    )
    grad, found = call(
        functools.partial(back_kernel, scale),
        [((chans * depth, own_width), F32), ((3, split * count), F32)],
        [
            ((inner + 2, 8 * chans, width), BF16),
            ((inner + 2, 32, width), F32),
            ((inner + 2, 16, width), F32),
            ((own_width // 128, chans * depth, 128), F32),
            ((inner - 1, 8 * chans, width), F32),
            pltpu.SemaphoreType.DMA((inner,)),
        ],
        (where, *messages, raw, raw2, slope, slope2, turned, point_back, near_ids, slope3),
        1,
        far=(slabs + 3,),
        away=(slabs + 3,),
    )
    colour = found[:, :count]
    if split == 2:
        other = lax.ppermute(grad, "view", pairing)
        colour = colour + lax.ppermute(found[:, count:], "view", pairing)
        grad = jnp.where(
            half == 0,
            jnp.concatenate([grad, other], axis=1),
            jnp.concatenate([other, grad], axis=1),
        )
    return (colour[None], grad.reshape(chans, depth, cells))


def solution(mesh):
    in_specs = (P(None, "slab", None), P(), P(), P(), P("view", None), P("view", None, "slab"))
    out_specs = (P("view", None, "slab"), P(None, "slab", None))
    return jax.shard_map(
        on_device, mesh=mesh, in_specs=in_specs, out_specs=out_specs, check_vma=False
    )
```
